32 devices in a mesh: dp: 8 (over y, x, core), mp: 4 (over z).
Axes of the slice: x: 2, y: 2, z: 4, core: 2. Of those that a mesh axis runs over, the one named last changes fastest.
Arguments:
- view_one: bfloat16 [1024, 4096], P('dp', 'mp'), may hold values from -400 to 400
- view_two: bfloat16 [1024, 4096], P('dp', 'mp'), may hold values from -400 to 400
- proj_weight: bfloat16 [4096, 4096], P(None, 'mp'), may hold values from -0.09375 to 0.09375
Outputs:
- grad_one: bfloat16 [1024, 4096], P('dp', 'mp')
- grad_two: bfloat16 [1024, 4096], P('dp', 'mp')
The draws below stay inside these ranges and needn't reach their ends.
All inputs are finite; a program needn't handle non-finite values.
Results may differ from the reference program's by a relative error of at most 0.025.
Values may be sent and summed in bfloat16 or wider, within the bound.
A program may use at most 128 MiB of HBM per device.

```python
import math
import jax
import jax.numpy as jnp
from jax import lax

E = 4096
K = 4096
B = 1024
N_MP = 4


def shared_parts(key):
    rows_key, cols_key, base_key = jax.random.split(key, 3)
    position = jnp.arange(B, dtype=jnp.float32)[:, None]
    rise = 1.0 + 2.0 * position / (B - 1)
    spread = jnp.exp(jax.random.uniform(rows_key, (B, 1), jnp.float32, 0.0, math.log(10.0)))
    column_scale = jnp.exp(jax.random.uniform(cols_key, (1, E), jnp.float32, math.log(0.3), math.log(3.0)))
    normal_base = jnp.clip(jax.random.normal(base_key, (B, E), jnp.float32), -4.0, 4.0)
    return (rise * spread, column_scale, normal_base)


def compose(key, row_scale, column_scale, base):
    return jnp.clip(row_scale * column_scale * base, -400.0, 400.0)


def draw_view_one(key, part):
    row_scale, column_scale, normal_base = shared_parts(key)
    key = jax.random.fold_in(key, 11)
    value = compose(key, row_scale, column_scale, normal_base)
    return value.astype(jnp.bfloat16)


def draw_view_two(key, part):
    row_scale, column_scale, normal_base = shared_parts(key)
    key = jax.random.fold_in(key, 12)
    own_key, col_key, off_key = jax.random.split(key, 3)
    second_scale = jnp.exp(jax.random.uniform(col_key, (1, E), jnp.float32, math.log(0.3), math.log(3.0)))
    noise = jnp.clip(jax.random.normal(own_key, (B, E), jnp.float32), -4.0, 4.0)
    value = compose(off_key, row_scale, second_scale, 0.8 * normal_base + 0.6 * noise)
    return value.astype(jnp.bfloat16)


def levels(key, shape, cuts, smallest, top_value):
    level = 1.0
    for axis_at, shards_of in cuts:
        heights = jax.random.uniform(jax.random.fold_in(jax.random.fold_in(key, 6), axis_at), (shards_of,), jnp.float32, smallest / len(cuts), top_value / len(cuts))
        level = level * jnp.repeat(jnp.exp(heights), shape[axis_at] // shards_of).reshape((-1,) + (1,) * (len(shape) - 1 - axis_at))
    return level


def gaussian(rng, shape, width, most, shards=(), kind=jnp.bfloat16):
    values = jax.random.normal(rng, shape, jnp.float32) * width
    if len(shards) > 0:
        values = levels(rng, shape, shards, -0.22, 0.18) * values
    return jnp.clip(values, min=-most, max=most).astype(kind)


def setup_inputs(seed: int = 0) -> dict:
    key_list = jax.random.split(jax.random.key(seed), 4)
    view_one = draw_view_one(jax.random.fold_in(key_list[3], 71), 0)
    view_two = draw_view_two(jax.random.fold_in(key_list[3], 71), 0)
    proj_weight = gaussian(key_list[2], (K, E), E ** -0.5, 0.09375, ((1, 4),))
    return {"view_one": view_one, "view_two": view_two, "proj_weight": proj_weight}


OFF_WEIGHT = 0.0125
EPSILON = 1e-05

def normalize(view):
    values = view.astype(jnp.float32)
    center = lax.optimization_barrier(jnp.mean(values, axis=0))
    centered = values - center
    variance = lax.optimization_barrier(jnp.mean(centered * centered, axis=0))
    inverse = lax.rsqrt(variance + EPSILON)
    return ((centered * inverse).astype(jnp.bfloat16), inverse)

def norm_backward(upstream, normed, inverse):
    normal_values = normed.astype(jnp.float32)
    mean_up = lax.optimization_barrier(jnp.mean(upstream, axis=0))
    mean_cross = lax.optimization_barrier(jnp.mean(upstream * normal_values, axis=0))
    return (inverse * (upstream - mean_up - normal_values * mean_cross)).astype(jnp.bfloat16)

def input_grad(delta, proj_weight):
    block = E // N_MP
    total = jnp.zeros((delta.shape[0], proj_weight.shape[0]), jnp.float32)
    for member in range(N_MP):
        piece = jnp.dot(delta[:, member * block:(member + 1) * block], proj_weight[:, member * block:(member + 1) * block].T, preferred_element_type=jnp.float32).astype(jnp.bfloat16)
        piece = lax.optimization_barrier(piece)
        total = total + piece.astype(jnp.float32)
    return total.astype(jnp.bfloat16)

def reference(view_one, view_two, proj_weight):
    row_count = view_one.shape[0]
    norm_one, inverse_one = normalize(view_one)
    norm_two, inverse_two = normalize(view_two)
    corr = jnp.dot(norm_one.T, norm_two, preferred_element_type=jnp.float32) / row_count
    row_ids = lax.broadcasted_iota(jnp.int32, (E, E), 0)
    col_ids = lax.broadcasted_iota(jnp.int32, (E, E), 1)
    grad_corr = jnp.where(row_ids == col_ids, -2.0 * (1.0 - corr), 2.0 * OFF_WEIGHT * corr).astype(jnp.bfloat16)
    up_one = jnp.dot(norm_two, grad_corr.T, preferred_element_type=jnp.float32)
    up_two = jnp.dot(norm_one, grad_corr, preferred_element_type=jnp.float32)
    delta_one = norm_backward(up_one, norm_one, inverse_one)
    delta_two = norm_backward(up_two, norm_two, inverse_two)
    return (input_grad(delta_one, proj_weight), input_grad(delta_two, proj_weight))
```

```python
import jax
import jax.numpy as jnp
from jax import lax
from jax.sharding import PartitionSpec as P

OFF_WEIGHT = 0.0125
EPSILON = 1e-05


def contract_rows(left, right):
    return lax.dot_general(
        left, right, (((0,), (0,)), ((), ())), preferred_element_type=jnp.float32
    )


def times_transposed(left, right):
    return lax.dot_general(
        left, right, (((1,), (1,)), ((), ())), preferred_element_type=jnp.float32
    )


def local(view_one, view_two, proj_weight):
    row_count, local_width = view_one.shape
    batch_devices = lax.axis_size("dp")
    total_rows = row_count * batch_devices
    first = view_one.astype(jnp.float32)
    second = view_two.astype(jnp.float32)
    sum_one, sum_two = lax.psum((jnp.sum(first, axis=0), jnp.sum(second, axis=0)), "dp")
    center_one = sum_one / total_rows
    center_two = sum_two / total_rows
    centered_one = first - center_one
    centered_two = second - center_two
    square_one, square_two = lax.psum(
        (
            jnp.sum(centered_one * centered_one, axis=0),
            jnp.sum(centered_two * centered_two, axis=0),
        ),
        "dp",
    )
    variance_one = square_one / total_rows
    variance_two = square_two / total_rows
    inverse_one = lax.rsqrt(variance_one + EPSILON)
    inverse_two = lax.rsqrt(variance_two + EPSILON)
    norm_one = (centered_one * inverse_one).astype(jnp.bfloat16)
    norm_two = (centered_two * inverse_two).astype(jnp.bfloat16)
    whole_two = lax.all_gather(norm_two, "mp", axis=1, tiled=True)
    total_width = whole_two.shape[1]
    block_index = lax.axis_index("mp")
    slab_index = lax.axis_index("dp")
    shard_cols = total_width // batch_devices
    corr_part = contract_rows(norm_one, whole_two)
    corr_shard = lax.psum_scatter(corr_part, "dp", scatter_dimension=1, tiled=True) / total_rows
    row_ids = block_index * local_width + lax.broadcasted_iota(
        jnp.int32, (local_width, shard_cols), 0
    )
    col_ids = slab_index * shard_cols + lax.broadcasted_iota(
        jnp.int32, (local_width, shard_cols), 1
    )
    grad_shard = jnp.where(
        row_ids == col_ids, -2.0 * (1.0 - corr_shard), 2.0 * OFF_WEIGHT * corr_shard
    ).astype(jnp.bfloat16)
    piece = lax.all_gather(grad_shard, "dp", axis=1, tiled=True)
    upper = times_transposed(whole_two, piece)
    fresh = jnp.dot(norm_one, piece, preferred_element_type=jnp.float32)
    up_two = lax.psum_scatter(
        fresh.astype(jnp.bfloat16), "mp", scatter_dimension=1, tiled=True
    ).astype(jnp.float32)
    normal_one = norm_one.astype(jnp.float32)
    normal_two = norm_two.astype(jnp.float32)
    mean_up_one, cross_one, mean_up_two, cross_two = lax.psum(
        (
            jnp.sum(upper, axis=0),
            jnp.sum(upper * normal_one, axis=0),
            jnp.sum(up_two, axis=0),
            jnp.sum(up_two * normal_two, axis=0),
        ),
        "dp",
    )
    delta_one = (
        inverse_one * (upper - mean_up_one / total_rows - normal_one * (cross_one / total_rows))
    ).astype(jnp.bfloat16)
    delta_two = (
        inverse_two * (up_two - mean_up_two / total_rows - normal_two * (cross_two / total_rows))
    ).astype(jnp.bfloat16)
    partial_one = times_transposed(delta_one, proj_weight)
    partial_two = times_transposed(delta_two, proj_weight)
    summed_one, summed_two = (
        lax.psum_scatter(
            partial_one.astype(jnp.bfloat16), "mp", scatter_dimension=1, tiled=True
        ).astype(jnp.float32),
        lax.psum_scatter(
            partial_two.astype(jnp.bfloat16), "mp", scatter_dimension=1, tiled=True
        ).astype(jnp.float32),
    )
    return (summed_one.astype(jnp.bfloat16), summed_two.astype(jnp.bfloat16))


def local_gram(view_one, view_two, proj_weight):
    row_count, local_width = view_one.shape
    total_rows = row_count * lax.axis_size("dp")
    mine = lax.axis_index("dp") * row_count
    views = lax.all_gather(jnp.stack([view_one, view_two]), "dp", axis=1, tiled=True)
    values = views.astype(jnp.float32)
    centered = values - jnp.mean(values, axis=1, keepdims=True)
    inverse = lax.rsqrt(jnp.mean(centered * centered, axis=1, keepdims=True) + EPSILON)
    norm = (centered * inverse).astype(jnp.bfloat16)
    own = lax.dynamic_slice_in_dim(norm, mine, row_count, axis=1)
    gram = lax.dot_general(
        own, norm, (((2,), (2,)), ((0,), (0,))), preferred_element_type=jnp.float32
    )
    gram = lax.psum(gram.astype(jnp.bfloat16), "mp")
    normal = norm.astype(jnp.float32)
    diagonal = jnp.mean(normal[0] * normal[1], axis=0)
    slope = 2.0 * (diagonal - 1.0) - 2.0 * OFF_WEIGHT * diagonal
    up = lax.dot_general(
        gram[::-1], norm, (((2,), (1,)), ((0,), (0,))), preferred_element_type=jnp.float32
    )
    own = own.astype(jnp.float32)
    up = up * (2.0 * OFF_WEIGHT / total_rows) + own[::-1] * slope
    mean_up, cross = lax.psum(
        (jnp.sum(up, axis=1, keepdims=True), jnp.sum(up * own, axis=1, keepdims=True)), "dp"
    )
    delta = (inverse * (up - mean_up / total_rows - own * (cross / total_rows))).astype(jnp.bfloat16)
    partial = lax.dot_general(
        delta, proj_weight, (((2,), (1,)), ((), ())), preferred_element_type=jnp.float32
    ).astype(jnp.bfloat16)
    summed = lax.psum_scatter(partial, "mp", scatter_dimension=2, tiled=True)
    return summed[0], summed[1]


def solution(mesh):
    placed = (P("dp", "mp"), P("dp", "mp"), P(None, "mp"))

    def whole(view_one, view_two, proj_weight):
        batch, features = view_one.shape
        form = local_gram if 2 * batch <= features else local
        return jax.shard_map(
            form, mesh=mesh, in_specs=placed, out_specs=(P("dp", "mp"), P("dp", "mp")), check_vma=False
        )(view_one, view_two, proj_weight)

    return whole
```

```python
import jax
import jax.numpy as jnp
from jax import lax
from jax.experimental import pallas as pl
from jax.experimental.pallas import tpu as pltpu
from jax.sharding import PartitionSpec as P

OFF_WEIGHT = 0.0125
EPSILON = 1e-05
MESH = pl.DeviceIdType.MESH
DP, MP = 8, 4
PARTS = 4


def times_t(left, right):
    return lax.dot_general(
        left, right, (((1,), (1,)), ((), ())), preferred_element_type=jnp.float32
    )


def fused(
    one_ref, two_ref, weight_hbm, grad_one_ref, grad_two_ref,
    weight, norm, stat, back, inverse_ref, diagonal, up, own_gram, from_end, from_mid, gram,
    delta, part, from_outer, from_inner,
    weight_sem, stat_s, stat_r, back_s, back_r, norm_s, norm_r,
    gram_s, end_r, mid_r, total_s, total_r, part_s, outer_r, inner_r,
):
    rows, width = one_ref.shape
    total_rows = rows * DP
    bf16, f32 = jnp.bfloat16, jnp.float32
    a, m = lax.axis_index("dp"), lax.axis_index("mp")
    core, along_x, along_y = lax.rem(a, 2), lax.rem(lax.div(a, 2), 2), lax.div(a, 4)

    def peer(r):
        at = a
        if r & 1:
            at = at + 1 - 2 * core
        if r & 2:
            at = at + 2 - 4 * along_x
        if r & 4:
            at = at + 4 - 8 * along_y
        return (at, m)

    low = m < 2
    is_mid = jnp.logical_and(m > 0, m < MP - 1)
    is_end = jnp.logical_not(is_mid)
    inner = (a, jnp.where(low, m + 1, m - 1))
    outer = (a, jnp.where(low, jnp.maximum(m - 1, 0), jnp.minimum(m + 1, MP - 1)))

    def remote(src, dst, send, recv, to):
        return pltpu.make_async_remote_copy(
            src_ref=src, dst_ref=dst, send_sem=send, recv_sem=recv, device_id=to, device_id_type=MESH
        )

    load = pltpu.make_async_copy(weight_hbm, weight, weight_sem)
    load.start()

    barrier = pltpu.get_barrier_semaphore()
    for r in range(1, DP):
        pl.semaphore_signal(barrier, inc=1, device_id=peer(r), device_id_type=MESH)
    pl.semaphore_signal(barrier, inc=1, device_id=inner, device_id_type=MESH)

    @pl.when(is_mid)
    def _():
        pl.semaphore_signal(barrier, inc=1, device_id=outer, device_id_type=MESH)

    for v, ref in enumerate((one_ref, two_ref)):
        x = ref[...].astype(f32)
        mean = jnp.sum(x, axis=0, keepdims=True) / rows
        x = x - mean
        stat[0, pl.ds(2 * v, 1)] = mean
        stat[0, pl.ds(2 * v + 1, 1)] = jnp.sum(x * x, axis=0, keepdims=True)

    pl.semaphore_wait(barrier, DP + jnp.where(is_mid, 1, 0))

    def stat_copy(r):
        return remote(stat.at[0], stat.at[r], stat_s.at[r], stat_r.at[r], peer(r))

    for r in range(DP - 1, 0, -1):
        stat_copy(r).start()
    for r in range(1, DP):
        stat_copy(r).wait_recv()
    for v, ref in enumerate((one_ref, two_ref)):
        means = [stat[r, pl.ds(2 * v, 1)] for r in range(DP)]
        mean = sum(means) / DP
        square = sum(stat[r, pl.ds(2 * v + 1, 1)] for r in range(DP))
        square = square + rows * sum((one - mean) * (one - mean) for one in means)
        inverse = lax.rsqrt(square / total_rows + EPSILON)
        inverse_ref[pl.ds(v, 1)] = inverse
        norm[v, pl.ds(0, rows)] = ((ref[...].astype(f32) - mean) * inverse).astype(bf16)

    def norm_copy(v, src, dst, via):
        return remote(
            norm.at[v, pl.ds(src * rows, rows)], norm.at[v, pl.ds(dst * rows, rows)],
            norm_s.at[dst, v], norm_r.at[dst, v], peer(via),
        )

    def norm_wait(v, slot):
        norm_copy(v, slot, slot, 1).wait_recv()

    sent = []

    def norm_send(v, src, dst, via):
        copy = norm_copy(v, src, dst, via)
        copy.start()
        sent.append(copy)

    norm_send(0, 0, 2, 2)
    norm_send(1, 0, 4, 4)
    norm_send(0, 0, 1, 1)
    norm_send(1, 0, 1, 1)
    norm_send(1, 0, 2, 2)
    norm_send(0, 0, 4, 4)

    chunks = ((0, 0), (1, 0), (0, 1), (1, 2), (1, 1), (0, 2), (0, 3), (1, 3))
    wide = 2 * rows

    def end_copy(k):
        return remote(own_gram.at[k], from_end.at[k], gram_s.at[k], end_r.at[k], inner)

    def mid_copy(k):
        return remote(own_gram.at[k], from_mid.at[k], gram_s.at[k], mid_r.at[k], inner)

    def total_copy(k):
        return remote(gram.at[k], gram.at[k], total_s.at[k], total_r.at[k], outer)

    def own(k):
        v, p = chunks[k]
        own_gram[k] = times_t(norm[v, pl.ds(0, rows)], norm[v, pl.ds(p * wide, wide)]).astype(bf16)

        @pl.when(is_end)
        def _():
            end_copy(k).start()

    def across(k):
        @pl.when(is_mid)
        def _():
            end_copy(k).wait_recv()
            own_gram[k] = (own_gram[k].astype(f32) + from_end[k].astype(f32)).astype(bf16)
            mid_copy(k).start()

    def back_out(k):
        @pl.when(is_mid)
        def _():
            mid_copy(k).wait_recv()
            gram[k] = (own_gram[k].astype(f32) + from_mid[k].astype(f32)).astype(bf16)
            total_copy(k).start()

    def use(k):
        v, p = chunks[k]

        @pl.when(is_end)
        def _():
            total_copy(k).wait_recv()

        product = jnp.dot(gram[k], norm[1 - v, pl.ds(p * wide, wide)], preferred_element_type=f32)
        if p == 0:
            up[1 - v] = product
        else:
            up[1 - v] += product

    def match(p):
        both = norm[0, pl.ds(p * wide, wide)].astype(f32) * norm[1, pl.ds(p * wide, wide)].astype(f32)
        both = jnp.sum(both, axis=0, keepdims=True)
        diagonal[pl.ds(0, 1)] = both if p == 0 else diagonal[pl.ds(0, 1)] + both

    norm_wait(0, 1)
    own(0)
    norm_wait(1, 1)
    own(1)
    across(0)
    across(1)
    match(0)
    back_out(0)
    back_out(1)

    norm_wait(0, 2)
    norm_send(0, 2, 6, 4)
    norm_send(0, 2, 3, 1)
    norm_wait(1, 4)
    norm_send(1, 4, 6, 2)
    norm_send(1, 4, 5, 1)
    norm_wait(0, 3)
    own(2)
    norm_wait(1, 5)
    own(3)
    use(0)
    use(1)
    across(2)
    across(3)
    back_out(2)
    back_out(3)

    norm_wait(1, 2)
    norm_send(1, 2, 3, 1)
    norm_wait(0, 4)
    norm_send(0, 4, 5, 1)
    norm_wait(1, 3)
    own(4)
    norm_wait(0, 5)
    own(5)
    use(2)
    use(3)
    across(4)
    across(5)
    match(1)
    match(2)
    back_out(4)
    back_out(5)

    norm_wait(0, 6)
    norm_send(0, 6, 7, 1)
    norm_wait(1, 6)
    norm_send(1, 6, 7, 1)
    norm_wait(0, 7)
    own(6)
    norm_wait(1, 7)
    own(7)
    across(6)
    across(7)
    use(4)
    use(5)
    match(3)
    back_out(6)
    back_out(7)
    use(6)
    use(7)

    diag = diagonal[pl.ds(0, 1)] / total_rows
    slope = 2.0 * (diag - 1.0) - 2.0 * OFF_WEIGHT * diag
    for v in range(2):
        mine = norm[v, pl.ds(0, rows)].astype(f32)
        other = norm[1 - v, pl.ds(0, rows)].astype(f32)
        value = up[v] * (2.0 * OFF_WEIGHT / total_rows) + other * slope
        up[v] = value
        back[0, pl.ds(2 * v, 1)] = jnp.sum(value, axis=0, keepdims=True)
        back[0, pl.ds(2 * v + 1, 1)] = jnp.sum(value * mine, axis=0, keepdims=True)

    def back_copy(r):
        return remote(back.at[0], back.at[r], back_s.at[r], back_r.at[r], peer(r))

    for r in range(DP - 1, 0, -1):
        back_copy(r).start()
    for r in range(1, DP):
        back_copy(r).wait_recv()
    for v in range(2):
        mean_up = sum(back[r, pl.ds(2 * v, 1)] for r in range(DP)) / total_rows
        cross = sum(back[r, pl.ds(2 * v + 1, 1)] for r in range(DP)) / total_rows
        mine = norm[v, pl.ds(0, rows)].astype(f32)
        delta[pl.ds(v * rows, rows)] = (
            inverse_ref[pl.ds(v, 1)] * (up[v] - mean_up - mine * cross)
        ).astype(bf16)

    load.wait()
    slim = width // PARTS

    def outward(j, c):
        return remote(part.at[j, c], from_outer.at[j, c], part_s.at[j, c], outer_r.at[j, c], inner)

    def over(j, c):
        return remote(part.at[j, c], from_inner.at[3 - j, c], part_s.at[j, c], inner_r.at[3 - j, c], inner)

    def homeward(c):
        return remote(part.at[0, c], from_inner.at[0, c], part_s.at[0, c], inner_r.at[0, c], outer)

    @pl.loop(0, MP * PARTS)
    def _(step):
        j = MP - 1 - lax.div(step, PARTS)
        c = lax.rem(step, PARTS)
        block = jnp.where(low, j, MP - 1 - j)
        start = pl.multiple_of(block * width + c * slim, slim)
        part[j, c] = times_t(delta[...], weight[pl.ds(start, slim)]).astype(bf16)

        @pl.when(jnp.logical_and(is_end, j > 0))
        def _():
            outward(j, c).start()

    def finish(c, value):
        value = value.astype(bf16)
        grad_one_ref[:, pl.ds(c * slim, slim)] = value[:rows]
        grad_two_ref[:, pl.ds(c * slim, slim)] = value[rows:]

    @pl.when(is_end)
    def _():
        for c in range(PARTS):
            homeward(c).wait_recv()
            finish(c, part[0, c].astype(f32) + from_inner[0, c].astype(f32))

    @pl.when(is_mid)
    def _():
        def pass_on(j, c):
            outward(j, c).wait_recv()
            part[j, c] = (part[j, c].astype(f32) + from_outer[j, c].astype(f32)).astype(bf16)
            over(j, c).start()

        def pass_home(c):
            over(3, c).wait_recv()
            part[0, c] = (part[0, c].astype(f32) + from_inner[0, c].astype(f32)).astype(bf16)
            homeward(c).start()

        order = [(3, c) for c in range(PARTS)] + [(2, c) for c in range(PARTS)]
        for at, (j, c) in enumerate(order):
            pass_on(j, c)
            if 1 <= at <= PARTS:
                pass_home(at - 1)
        for c in range(PARTS):
            over(2, c).wait_recv()
            outward(1, c).wait_recv()
            finish(
                c, part[1, c].astype(f32) + from_outer[1, c].astype(f32) + from_inner[1, c].astype(f32)
            )

    for r in range(1, DP):
        stat_copy(r).wait_send()
        back_copy(r).wait_send()
    for copy in sent:
        copy.wait_send()
    for k in range(len(chunks)):
        end_copy(k).wait_send()

    @pl.when(is_mid)
    def _():
        for k in range(len(chunks)):
            total_copy(k).wait_send()
        for c in range(PARTS):
            for j in (0, 2, 3):
                outward(j, c).wait_send()

    @pl.when(is_end)
    def _():
        for c in range(PARTS):
            for j in (1, 2, 3):
                outward(j, c).wait_send()


def local_fused(view_one, view_two, proj_weight):
    rows, width = view_one.shape
    bf16, f32 = jnp.bfloat16, jnp.float32
    dma = pltpu.SemaphoreType.DMA
    slim = width // PARTS
    out = jax.ShapeDtypeStruct((rows, width), bf16)
    vmem = pl.BlockSpec(memory_space=pltpu.VMEM)
    return pl.pallas_call(
        fused,
        out_shape=(out, out),
        in_specs=[vmem, vmem, pl.BlockSpec(memory_space=pl.ANY)],
        out_specs=(vmem, vmem),
        scratch_shapes=[
            pltpu.VMEM(proj_weight.shape, bf16),
            pltpu.VMEM((2, DP * rows, width), bf16),
            pltpu.VMEM((DP, 4, width), f32),
            pltpu.VMEM((DP, 4, width), f32),
            pltpu.VMEM((8, width), f32),
            pltpu.VMEM((8, width), f32),
            pltpu.VMEM((2, rows, width), f32),
            pltpu.VMEM((8, rows, 2 * rows), bf16),
            pltpu.VMEM((8, rows, 2 * rows), bf16),
            pltpu.VMEM((8, rows, 2 * rows), bf16),
            pltpu.VMEM((8, rows, 2 * rows), bf16),
            pltpu.VMEM((2 * rows, width), bf16),
            pltpu.VMEM((MP, PARTS, 2 * rows, slim), bf16),
            pltpu.VMEM((MP, PARTS, 2 * rows, slim), bf16),
            pltpu.VMEM((2, PARTS, 2 * rows, slim), bf16),
            dma(()),
            dma((DP,)), dma((DP,)), dma((DP,)), dma((DP,)),
            dma((DP, 2)), dma((DP, 2)),
            dma((8,)), dma((8,)), dma((8,)), dma((8,)), dma((8,)),
            dma((MP, PARTS)), dma((MP, PARTS)), dma((2, PARTS)),
        ],
        compiler_params=pltpu.CompilerParams(
            collective_id=0, has_side_effects=True, vmem_limit_bytes=48 * 1024 * 1024
        ),
        cost_estimate=pl.CostEstimate(
            flops=4 * rows * width * (2 * DP * rows + MP * width),
            bytes_accessed=2 * (MP * width * width + 4 * rows * width),
            transcendentals=0,
        ),
    )(view_one, view_two, proj_weight)


def contract_rows(left, right):
    return lax.dot_general(
        left, right, (((0,), (0,)), ((), ())), preferred_element_type=jnp.float32
    )


def times_transposed(left, right):
    return lax.dot_general(
        left, right, (((1,), (1,)), ((), ())), preferred_element_type=jnp.float32
    )


def local(view_one, view_two, proj_weight):
    row_count, local_width = view_one.shape
    batch_devices = lax.axis_size("dp")
    total_rows = row_count * batch_devices
    first = view_one.astype(jnp.float32)
    second = view_two.astype(jnp.float32)
    sum_one, sum_two = lax.psum((jnp.sum(first, axis=0), jnp.sum(second, axis=0)), "dp")
    center_one = sum_one / total_rows
    center_two = sum_two / total_rows
    centered_one = first - center_one
    centered_two = second - center_two
    square_one, square_two = lax.psum(
        (
            jnp.sum(centered_one * centered_one, axis=0),
            jnp.sum(centered_two * centered_two, axis=0),
        ),
        "dp",
    )
    variance_one = square_one / total_rows
    variance_two = square_two / total_rows
    inverse_one = lax.rsqrt(variance_one + EPSILON)
    inverse_two = lax.rsqrt(variance_two + EPSILON)
    norm_one = (centered_one * inverse_one).astype(jnp.bfloat16)
    norm_two = (centered_two * inverse_two).astype(jnp.bfloat16)
    whole_two = lax.all_gather(norm_two, "mp", axis=1, tiled=True)
    total_width = whole_two.shape[1]
    block_index = lax.axis_index("mp")
    slab_index = lax.axis_index("dp")
    shard_cols = total_width // batch_devices
    corr_part = contract_rows(norm_one, whole_two)
    corr_shard = lax.psum_scatter(corr_part, "dp", scatter_dimension=1, tiled=True) / total_rows
    row_ids = block_index * local_width + lax.broadcasted_iota(
        jnp.int32, (local_width, shard_cols), 0
    )
    col_ids = slab_index * shard_cols + lax.broadcasted_iota(
        jnp.int32, (local_width, shard_cols), 1
    )
    grad_shard = jnp.where(
        row_ids == col_ids, -2.0 * (1.0 - corr_shard), 2.0 * OFF_WEIGHT * corr_shard
    ).astype(jnp.bfloat16)
    piece = lax.all_gather(grad_shard, "dp", axis=1, tiled=True)
    upper = times_transposed(whole_two, piece)
    fresh = jnp.dot(norm_one, piece, preferred_element_type=jnp.float32)
    up_two = lax.psum_scatter(
        fresh.astype(jnp.bfloat16), "mp", scatter_dimension=1, tiled=True
    ).astype(jnp.float32)
    normal_one = norm_one.astype(jnp.float32)
    normal_two = norm_two.astype(jnp.float32)
    mean_up_one, cross_one, mean_up_two, cross_two = lax.psum(
        (
            jnp.sum(upper, axis=0),
            jnp.sum(upper * normal_one, axis=0),
            jnp.sum(up_two, axis=0),
            jnp.sum(up_two * normal_two, axis=0),
        ),
        "dp",
    )
    delta_one = (
        inverse_one * (upper - mean_up_one / total_rows - normal_one * (cross_one / total_rows))
    ).astype(jnp.bfloat16)
    delta_two = (
        inverse_two * (up_two - mean_up_two / total_rows - normal_two * (cross_two / total_rows))
    ).astype(jnp.bfloat16)
    partial_one = times_transposed(delta_one, proj_weight)
    partial_two = times_transposed(delta_two, proj_weight)
    summed_one, summed_two = (
        lax.psum_scatter(
            partial_one.astype(jnp.bfloat16), "mp", scatter_dimension=1, tiled=True
        ).astype(jnp.float32),
        lax.psum_scatter(
            partial_two.astype(jnp.bfloat16), "mp", scatter_dimension=1, tiled=True
        ).astype(jnp.float32),
    )
    return (summed_one.astype(jnp.bfloat16), summed_two.astype(jnp.bfloat16))


def solution(mesh):
    placed = (P("dp", "mp"), P("dp", "mp"), P(None, "mp"))

    def whole(view_one, view_two, proj_weight):
        batch, features = view_one.shape
        suits = dict(mesh.shape) == {"dp": DP, "mp": MP}
        suits = suits and batch % (DP * 128) == 0 and 2 * batch <= features and features <= 4096
        return jax.shard_map(
            local_fused if suits else local,
            mesh=mesh, in_specs=placed, out_specs=(P("dp", "mp"), P("dp", "mp")), check_vma=False,
        )(view_one, view_two, proj_weight)

    return whole
```

```python
import jax
import jax.numpy as jnp
from jax import lax
from jax.experimental import pallas as pl
from jax.experimental.pallas import tpu as pltpu
from jax.sharding import PartitionSpec as P

OFF_WEIGHT = 0.0125
EPSILON = 1e-05
MESH = pl.DeviceIdType.MESH
DP, MP = 8, 4
AHEAD = 2
PARTS = 4


def times_t(left, right):
    return lax.dot_general(
        left, right, (((1,), (1,)), ((), ())), preferred_element_type=jnp.float32
    )


def fused(
    one_hbm, two_hbm, weight_hbm, grad_one_ref, grad_two_ref,
    views, weight, norm, stat, back, inverse_ref, diagonal, up, own_gram, from_end, from_mid, gram,
    delta, part, from_outer, from_inner,
    view_sem, weight_sem, stat_s, stat_r, back_s, back_r, norm_s, norm_r,
    gram_s, end_r, mid_r, total_s, total_r, part_s, outer_r, inner_r,
):
    _, rows, width = views.shape
    total_rows = rows * DP
    bf16, f32 = jnp.bfloat16, jnp.float32
    a, m = lax.axis_index("dp"), lax.axis_index("mp")
    core, along_x, along_y = lax.rem(a, 2), lax.rem(lax.div(a, 2), 2), lax.div(a, 4)

    def peer(r):
        at = a
        if r & 1:
            at = at + 1 - 2 * core
        if r & 2:
            at = at + 2 - 4 * along_x
        if r & 4:
            at = at + 4 - 8 * along_y
        return (at, m)

    low = m < 2
    is_mid = jnp.logical_and(m > 0, m < MP - 1)
    is_end = jnp.logical_not(is_mid)
    inner = (a, jnp.where(low, m + 1, m - 1))
    outer = (a, jnp.where(low, jnp.maximum(m - 1, 0), jnp.minimum(m + 1, MP - 1)))

    def remote(src, dst, send, recv, to):
        return pltpu.make_async_remote_copy(
            src_ref=src, dst_ref=dst, send_sem=send, recv_sem=recv, device_id=to, device_id_type=MESH
        )

    fetch = [
        pltpu.make_async_copy(ref, views.at[v], view_sem.at[v])
        for v, ref in enumerate((one_hbm, two_hbm))
    ]
    for copy in fetch:
        copy.start()
    load = pltpu.make_async_copy(weight_hbm, weight, weight_sem)
    load.start()

    barrier = pltpu.get_barrier_semaphore()
    for r in range(1, DP):
        pl.semaphore_signal(barrier, inc=1, device_id=peer(r), device_id_type=MESH)
    pl.semaphore_signal(barrier, inc=1, device_id=inner, device_id_type=MESH)

    @pl.when(is_mid)
    def _():
        pl.semaphore_signal(barrier, inc=1, device_id=outer, device_id_type=MESH)

    for v in range(2):
        fetch[v].wait()
        x = views[v].astype(f32)
        mean = jnp.sum(x, axis=0, keepdims=True) / rows
        x = x - mean
        stat[0, pl.ds(2 * v, 1)] = mean
        stat[0, pl.ds(2 * v + 1, 1)] = jnp.sum(x * x, axis=0, keepdims=True)

    pl.semaphore_wait(barrier, DP + jnp.where(is_mid, 1, 0))

    def stat_copy(r):
        return remote(stat.at[0], stat.at[r], stat_s.at[r], stat_r.at[r], peer(r))

    for r in range(DP - 1, 0, -1):
        stat_copy(r).start()
    for r in range(1, DP):
        stat_copy(r).wait_recv()
    for v in range(2):
        means = [stat[r, pl.ds(2 * v, 1)] for r in range(DP)]
        mean = sum(means) / DP
        square = sum(stat[r, pl.ds(2 * v + 1, 1)] for r in range(DP))
        square = square + rows * sum((one - mean) * (one - mean) for one in means)
        inverse = lax.rsqrt(square / total_rows + EPSILON)
        inverse_ref[pl.ds(v, 1)] = inverse
        norm[v, pl.ds(0, rows)] = ((views[v].astype(f32) - mean) * inverse).astype(bf16)

    def norm_copy(v, src, dst, via):
        return remote(
            norm.at[v, pl.ds(src * rows, rows)], norm.at[v, pl.ds(dst * rows, rows)],
            norm_s.at[dst, v], norm_r.at[dst, v], peer(via),
        )

    def norm_wait(v, slot):
        norm_copy(v, slot, slot, 1).wait_recv()

    sent = []

    def norm_send(v, src, dst, via):
        copy = norm_copy(v, src, dst, via)
        copy.start()
        sent.append(copy)

    norm_send(0, 0, 2, 2)
    norm_send(1, 0, 4, 4)
    norm_send(0, 0, 1, 1)
    norm_send(1, 0, 1, 1)
    norm_send(1, 0, 2, 2)
    norm_send(0, 0, 4, 4)

    chunks = ((0, 0), (1, 0), (0, 1), (1, 2), (1, 1), (0, 2), (0, 3), (1, 3))
    wide = 2 * rows

    def end_copy(k):
        return remote(own_gram.at[k], from_end.at[k], gram_s.at[k], end_r.at[k], inner)

    def mid_copy(k):
        return remote(own_gram.at[k], from_mid.at[k], gram_s.at[k], mid_r.at[k], inner)

    def total_copy(k):
        return remote(gram.at[k], gram.at[k], total_s.at[k], total_r.at[k], outer)

    def own(k):
        v, p = chunks[k]
        own_gram[k] = times_t(norm[v, pl.ds(0, rows)], norm[v, pl.ds(p * wide, wide)]).astype(bf16)

        @pl.when(is_end)
        def _():
            end_copy(k).start()

    def across(k):
        @pl.when(is_mid)
        def _():
            end_copy(k).wait_recv()
            own_gram[k] = (own_gram[k].astype(f32) + from_end[k].astype(f32)).astype(bf16)
            mid_copy(k).start()

    def back_out(k):
        @pl.when(is_mid)
        def _():
            mid_copy(k).wait_recv()
            gram[k] = (own_gram[k].astype(f32) + from_mid[k].astype(f32)).astype(bf16)
            total_copy(k).start()

    def use(k):
        v, p = chunks[k]

        @pl.when(is_end)
        def _():
            total_copy(k).wait_recv()

        product = jnp.dot(gram[k], norm[1 - v, pl.ds(p * wide, wide)], preferred_element_type=f32)
        if p == 0:
            up[1 - v] = product
        else:
            up[1 - v] += product

    def match(p):
        both = norm[0, pl.ds(p * wide, wide)].astype(f32) * norm[1, pl.ds(p * wide, wide)].astype(f32)
        both = jnp.sum(both, axis=0, keepdims=True)
        diagonal[pl.ds(0, 1)] = both if p == 0 else diagonal[pl.ds(0, 1)] + both

    norm_wait(0, 1)
    own(0)
    norm_wait(1, 1)
    own(1)
    across(0)
    across(1)
    match(0)
    back_out(0)
    back_out(1)

    norm_wait(0, 2)
    norm_send(0, 2, 6, 4)
    norm_send(0, 2, 3, 1)
    norm_wait(1, 4)
    norm_send(1, 4, 6, 2)
    norm_send(1, 4, 5, 1)
    norm_wait(0, 3)
    own(2)
    norm_wait(1, 5)
    own(3)
    use(0)
    use(1)
    across(2)
    across(3)
    back_out(2)
    back_out(3)

    norm_wait(1, 2)
    norm_send(1, 2, 3, 1)
    norm_wait(0, 4)
    norm_send(0, 4, 5, 1)
    norm_wait(1, 3)
    own(4)
    norm_wait(0, 5)
    own(5)
    use(2)
    use(3)
    across(4)
    across(5)
    match(1)
    match(2)
    back_out(4)
    back_out(5)

    norm_wait(0, 6)
    norm_send(0, 6, 7, 1)
    norm_wait(1, 6)
    norm_send(1, 6, 7, 1)
    norm_wait(0, 7)
    own(6)
    norm_wait(1, 7)
    own(7)
    across(6)
    across(7)
    use(4)
    use(5)
    match(3)
    back_out(6)
    back_out(7)
    use(6)
    use(7)

    diag = diagonal[pl.ds(0, 1)] / total_rows
    slope = 2.0 * (diag - 1.0) - 2.0 * OFF_WEIGHT * diag
    for v in range(2):
        mine = norm[v, pl.ds(0, rows)].astype(f32)
        other = norm[1 - v, pl.ds(0, rows)].astype(f32)
        value = up[v] * (2.0 * OFF_WEIGHT / total_rows) + other * slope
        up[v] = value
        back[0, pl.ds(2 * v, 1)] = jnp.sum(value, axis=0, keepdims=True)
        back[0, pl.ds(2 * v + 1, 1)] = jnp.sum(value * mine, axis=0, keepdims=True)

    def back_copy(r):
        return remote(back.at[0], back.at[r], back_s.at[r], back_r.at[r], peer(r))

    for r in range(DP - 1, 0, -1):
        back_copy(r).start()
    for r in range(1, DP):
        back_copy(r).wait_recv()
    for v in range(2):
        mean_up = sum(back[r, pl.ds(2 * v, 1)] for r in range(DP)) / total_rows
        cross = sum(back[r, pl.ds(2 * v + 1, 1)] for r in range(DP)) / total_rows
        mine = norm[v, pl.ds(0, rows)].astype(f32)
        delta[pl.ds(v * rows, rows)] = (
            inverse_ref[pl.ds(v, 1)] * (up[v] - mean_up - mine * cross)
        ).astype(bf16)

    load.wait()
    slim = width // PARTS

    def outward(j, c):
        return remote(part.at[j, c], from_outer.at[j, c], part_s.at[j, c], outer_r.at[j, c], inner)

    def over(j, c):
        return remote(part.at[j, c], from_inner.at[3 - j, c], part_s.at[j, c], inner_r.at[3 - j, c], inner)

    def homeward(c):
        return remote(part.at[0, c], from_inner.at[0, c], part_s.at[0, c], inner_r.at[0, c], outer)

    @pl.loop(0, MP * PARTS)
    def _(step):
        j = MP - 1 - lax.div(step, PARTS)
        c = lax.rem(step, PARTS)
        block = jnp.where(low, j, MP - 1 - j)
        start = pl.multiple_of(block * width + c * slim, slim)
        part[j, c] = times_t(delta[...], weight[pl.ds(start, slim)]).astype(bf16)

        @pl.when(jnp.logical_and(is_end, j > 0))
        def _():
            @pl.when(step >= AHEAD)
            def _():
                before = step - AHEAD
                outward(MP - 1 - lax.div(before, PARTS), lax.rem(before, PARTS)).wait_send()

            outward(j, c).start()

    def finish(c, value):
        value = value.astype(bf16)
        grad_one_ref[:, pl.ds(c * slim, slim)] = value[:rows]
        grad_two_ref[:, pl.ds(c * slim, slim)] = value[rows:]

    @pl.when(is_end)
    def _():
        for c in range(PARTS):
            homeward(c).wait_recv()
            finish(c, part[0, c].astype(f32) + from_inner[0, c].astype(f32))

    @pl.when(is_mid)
    def _():
        def pass_on(j, c):
            outward(j, c).wait_recv()
            part[j, c] = (part[j, c].astype(f32) + from_outer[j, c].astype(f32)).astype(bf16)
            over(j, c).start()

        def pass_home(c):
            over(3, c).wait_recv()
            part[0, c] = (part[0, c].astype(f32) + from_inner[0, c].astype(f32)).astype(bf16)
            homeward(c).start()

        order = [(3, c) for c in range(PARTS)] + [(2, c) for c in range(PARTS)]
        for at, (j, c) in enumerate(order):
            pass_on(j, c)
            if 1 <= at <= PARTS:
                pass_home(at - 1)
        for c in range(PARTS):
            over(2, c).wait_recv()
            outward(1, c).wait_recv()
            finish(
                c, part[1, c].astype(f32) + from_outer[1, c].astype(f32) + from_inner[1, c].astype(f32)
            )

    for r in range(1, DP):
        stat_copy(r).wait_send()
        back_copy(r).wait_send()
    for copy in sent:
        copy.wait_send()
    for k in range(len(chunks)):
        end_copy(k).wait_send()

    @pl.when(is_mid)
    def _():
        for k in range(len(chunks)):
            total_copy(k).wait_send()
        for c in range(PARTS):
            for j in (0, 2, 3):
                outward(j, c).wait_send()

    @pl.when(is_end)
    def _():
        for step in range((MP - 1) * PARTS - AHEAD, (MP - 1) * PARTS):
            outward(MP - 1 - step // PARTS, step % PARTS).wait_send()


def local_fused(view_one, view_two, proj_weight):
    rows, width = view_one.shape
    bf16, f32 = jnp.bfloat16, jnp.float32
    dma = pltpu.SemaphoreType.DMA
    slim = width // PARTS
    out = jax.ShapeDtypeStruct((rows, width), bf16)
    vmem = pl.BlockSpec(memory_space=pltpu.VMEM)
    return pl.pallas_call(
        fused,
        out_shape=(out, out),
        in_specs=[pl.BlockSpec(memory_space=pl.ANY)] * 3,
        out_specs=(vmem, vmem),
        scratch_shapes=[
            pltpu.VMEM((2, rows, width), bf16),
            pltpu.VMEM(proj_weight.shape, bf16),
            pltpu.VMEM((2, DP * rows, width), bf16),
            pltpu.VMEM((DP, 4, width), f32),
            pltpu.VMEM((DP, 4, width), f32),
            pltpu.VMEM((8, width), f32),
            pltpu.VMEM((8, width), f32),
            pltpu.VMEM((2, rows, width), f32),
            pltpu.VMEM((8, rows, 2 * rows), bf16),
            pltpu.VMEM((8, rows, 2 * rows), bf16),
            pltpu.VMEM((8, rows, 2 * rows), bf16),
            pltpu.VMEM((8, rows, 2 * rows), bf16),
            pltpu.VMEM((2 * rows, width), bf16),
            pltpu.VMEM((MP, PARTS, 2 * rows, slim), bf16),
            pltpu.VMEM((MP, PARTS, 2 * rows, slim), bf16),
            pltpu.VMEM((2, PARTS, 2 * rows, slim), bf16),
            dma((2,)),
            dma(()),
            dma((DP,)), dma((DP,)), dma((DP,)), dma((DP,)),
            dma((DP, 2)), dma((DP, 2)),
            dma((8,)), dma((8,)), dma((8,)), dma((8,)), dma((8,)),
            dma((MP, PARTS)), dma((MP, PARTS)), dma((2, PARTS)),
        ],
        compiler_params=pltpu.CompilerParams(
            collective_id=0, has_side_effects=True, vmem_limit_bytes=48 * 1024 * 1024
        ),
        cost_estimate=pl.CostEstimate(
            flops=4 * rows * width * (2 * DP * rows + MP * width),
            bytes_accessed=2 * (MP * width * width + 4 * rows * width),
            transcendentals=0,
        ),
    )(view_one, view_two, proj_weight)


def contract_rows(left, right):
    return lax.dot_general(
        left, right, (((0,), (0,)), ((), ())), preferred_element_type=jnp.float32
    )


def times_transposed(left, right):
    return lax.dot_general(
        left, right, (((1,), (1,)), ((), ())), preferred_element_type=jnp.float32
    )


def local(view_one, view_two, proj_weight):
    row_count, local_width = view_one.shape
    batch_devices = lax.axis_size("dp")
    total_rows = row_count * batch_devices
    first = view_one.astype(jnp.float32)
    second = view_two.astype(jnp.float32)
    sum_one, sum_two = lax.psum((jnp.sum(first, axis=0), jnp.sum(second, axis=0)), "dp")
    center_one = sum_one / total_rows
    center_two = sum_two / total_rows
    centered_one = first - center_one
    centered_two = second - center_two
    square_one, square_two = lax.psum(
        (
            jnp.sum(centered_one * centered_one, axis=0),
            jnp.sum(centered_two * centered_two, axis=0),
        ),
        "dp",
    )
    variance_one = square_one / total_rows
    variance_two = square_two / total_rows
    inverse_one = lax.rsqrt(variance_one + EPSILON)
    inverse_two = lax.rsqrt(variance_two + EPSILON)
    norm_one = (centered_one * inverse_one).astype(jnp.bfloat16)
    norm_two = (centered_two * inverse_two).astype(jnp.bfloat16)
    whole_two = lax.all_gather(norm_two, "mp", axis=1, tiled=True)
    total_width = whole_two.shape[1]
    block_index = lax.axis_index("mp")
    slab_index = lax.axis_index("dp")
    shard_cols = total_width // batch_devices
    corr_part = contract_rows(norm_one, whole_two)
    corr_shard = lax.psum_scatter(corr_part, "dp", scatter_dimension=1, tiled=True) / total_rows
    row_ids = block_index * local_width + lax.broadcasted_iota(
        jnp.int32, (local_width, shard_cols), 0
    )
    col_ids = slab_index * shard_cols + lax.broadcasted_iota(
        jnp.int32, (local_width, shard_cols), 1
    )
    grad_shard = jnp.where(
        row_ids == col_ids, -2.0 * (1.0 - corr_shard), 2.0 * OFF_WEIGHT * corr_shard
    ).astype(jnp.bfloat16)
    piece = lax.all_gather(grad_shard, "dp", axis=1, tiled=True)
    upper = times_transposed(whole_two, piece)
    fresh = jnp.dot(norm_one, piece, preferred_element_type=jnp.float32)
    up_two = lax.psum_scatter(
        fresh.astype(jnp.bfloat16), "mp", scatter_dimension=1, tiled=True
    ).astype(jnp.float32)
    normal_one = norm_one.astype(jnp.float32)
    normal_two = norm_two.astype(jnp.float32)
    mean_up_one, cross_one, mean_up_two, cross_two = lax.psum(
        (
            jnp.sum(upper, axis=0),
            jnp.sum(upper * normal_one, axis=0),
            jnp.sum(up_two, axis=0),
            jnp.sum(up_two * normal_two, axis=0),
        ),
        "dp",
    )
    delta_one = (
        inverse_one * (upper - mean_up_one / total_rows - normal_one * (cross_one / total_rows))
    ).astype(jnp.bfloat16)
    delta_two = (
        inverse_two * (up_two - mean_up_two / total_rows - normal_two * (cross_two / total_rows))
    ).astype(jnp.bfloat16)
    partial_one = times_transposed(delta_one, proj_weight)
    partial_two = times_transposed(delta_two, proj_weight)
    summed_one, summed_two = (
        lax.psum_scatter(
            partial_one.astype(jnp.bfloat16), "mp", scatter_dimension=1, tiled=True
        ).astype(jnp.float32),
        lax.psum_scatter(
            partial_two.astype(jnp.bfloat16), "mp", scatter_dimension=1, tiled=True
        ).astype(jnp.float32),
    )
    return (summed_one.astype(jnp.bfloat16), summed_two.astype(jnp.bfloat16))


def solution(mesh):
    placed = (P("dp", "mp"), P("dp", "mp"), P(None, "mp"))

    def whole(view_one, view_two, proj_weight):
        batch, features = view_one.shape
        suits = dict(mesh.shape) == {"dp": DP, "mp": MP}
        suits = suits and batch % (DP * 128) == 0 and 2 * batch <= features and features <= 4096
        return jax.shard_map(
            local_fused if suits else local,
            mesh=mesh, in_specs=placed, out_specs=(P("dp", "mp"), P("dp", "mp")), check_vma=False,
        )(view_one, view_two, proj_weight)

    return whole
```

```python
import jax
import jax.numpy as jnp
from jax import lax
from jax.experimental import pallas as pl
from jax.experimental.pallas import tpu as pltpu
from jax.sharding import PartitionSpec as P

OFF_WEIGHT = 0.0125
EPSILON = 1e-05
MESH = pl.DeviceIdType.MESH
DP, MP = 8, 4
VMEM_MIB = 60
PARTS = 4


def times_t(left, right):
    return lax.dot_general(
        left, right, (((1,), (1,)), ((), ())), preferred_element_type=jnp.float32
    )


def fused(
    one_hbm, two_hbm, weight_hbm, grad_one_ref, grad_two_ref,
    weight, raw, norm, stat, back, inverse_ref, mean_ref, diagonal, up, own_gram, from_end, from_mid,
    gram, delta, part, from_outer, from_inner,
    view_sem, weight_sem, stat_s, stat_r, back_s, back_r, raw_s, raw_r,
    gram_s, end_r, mid_r, total_s, total_r, part_s, outer_r, inner_r,
):
    rows, width = one_hbm.shape
    total_rows = rows * DP
    half = rows // 2
    bf16, f32 = jnp.bfloat16, jnp.float32
    a, m = lax.axis_index("dp"), lax.axis_index("mp")
    core, along_x, along_y = lax.rem(a, 2), lax.rem(lax.div(a, 2), 2), lax.div(a, 4)

    def peer(r):
        at = a
        if r & 1:
            at = at + 1 - 2 * core
        if r & 2:
            at = at + 2 - 4 * along_x
        if r & 4:
            at = at + 4 - 8 * along_y
        return (at, m)

    low = m < 2
    is_mid = jnp.logical_and(m > 0, m < MP - 1)
    is_end = jnp.logical_not(is_mid)
    inner = (a, jnp.where(low, m + 1, m - 1))
    outer = (a, jnp.where(low, jnp.maximum(m - 1, 0), jnp.minimum(m + 1, MP - 1)))

    def remote(src, dst, send, recv, to):
        return pltpu.make_async_remote_copy(
            src_ref=src, dst_ref=dst, send_sem=send, recv_sem=recv, device_id=to, device_id_type=MESH
        )

    fetch = [
        pltpu.make_async_copy(ref, raw.at[v, pl.ds(0, rows)], view_sem.at[v])
        for v, ref in enumerate((one_hbm, two_hbm))
    ]
    fetch[1].start()
    fetch[0].start()
    load = pltpu.make_async_copy(weight_hbm, weight, weight_sem)
    load.start()

    barrier = pltpu.get_barrier_semaphore()
    for r in range(1, DP):
        pl.semaphore_signal(barrier, inc=1, device_id=peer(r), device_id_type=MESH)
    pl.semaphore_signal(barrier, inc=1, device_id=inner, device_id_type=MESH)

    @pl.when(is_mid)
    def _():
        pl.semaphore_signal(barrier, inc=1, device_id=outer, device_id_type=MESH)

    def raw_copy(v, src, dst, via, h=None):
        size = rows if h is None else half
        skip = 0 if h is None else h * half
        return remote(
            raw.at[v, pl.ds(src * rows + skip, size)], raw.at[v, pl.ds(dst * rows + skip, size)],
            raw_s.at[dst, v, h or 0], raw_r.at[dst, v, h or 0], peer(via),
        )

    def got(v, slot, h=None):
        raw_copy(v, slot, slot, 1, h).wait_recv()

    sent = []

    def give(v, src, dst, via, h=None):
        copy = raw_copy(v, src, dst, via, h)
        copy.start()
        sent.append(copy)

    def give_own(v):
        give(v, 0, 2, 2, 0)
        give(v, 0, 4, 4, 1)
        give(v, 0, 1, 1)
        give(v, 0, 2, 2, 1)
        give(v, 0, 4, 4, 0)

    def give_across(v):
        got(v, 2, 0)
        give(v, 2, 6, 4, 0)
        got(v, 4, 1)
        give(v, 4, 6, 2, 1)

    def block_stat(v):
        x = raw[v, pl.ds(0, rows)].astype(f32)
        mean = jnp.sum(x, axis=0, keepdims=True) / rows
        x = x - mean
        stat[0, pl.ds(2 * v, 1)] = mean
        stat[0, pl.ds(2 * v + 1, 1)] = jnp.sum(x * x, axis=0, keepdims=True)

    def stat_copy(r):
        return remote(stat.at[0], stat.at[r], stat_s.at[r], stat_r.at[r], peer(r))

    for v in (1, 0):
        fetch[v].wait()
        block_stat(v)
    pl.semaphore_wait(barrier, DP + jnp.where(is_mid, 1, 0))
    for r in range(DP - 1, 0, -1):
        stat_copy(r).start()
    give_own(1)
    for r in range(1, DP):
        stat_copy(r).wait_recv()
    for v in range(2):
        means = [stat[r, pl.ds(2 * v, 1)] for r in range(DP)]
        mean = sum(means) / DP
        square = sum(stat[r, pl.ds(2 * v + 1, 1)] for r in range(DP))
        square = square + rows * sum((one - mean) * (one - mean) for one in means)
        mean_ref[pl.ds(v, 1)] = mean
        inverse_ref[pl.ds(v, 1)] = lax.rsqrt(square / total_rows + EPSILON)

    def normalize(v, slot):
        x = raw[v, pl.ds(slot * rows, rows)].astype(f32)
        norm[v, pl.ds(slot * rows, rows)] = (
            (x - mean_ref[pl.ds(v, 1)]) * inverse_ref[pl.ds(v, 1)]
        ).astype(bf16)

    chunks = ((1, 0), (1, 1), (1, 2), (1, 3), (0, 0), (0, 1), (0, 2), (0, 3))
    wide = 2 * rows

    def end_copy(k):
        return remote(own_gram.at[k], from_end.at[k], gram_s.at[k], end_r.at[k], inner)

    def mid_copy(k):
        return remote(own_gram.at[k], from_mid.at[k], gram_s.at[k], mid_r.at[k], inner)

    def total_copy(k):
        return remote(gram.at[k], gram.at[k], total_s.at[k], total_r.at[k], outer)

    def own(k):
        v, p = chunks[k]
        own_gram[k] = times_t(norm[v, pl.ds(0, rows)], norm[v, pl.ds(p * wide, wide)]).astype(bf16)

        @pl.when(is_end)
        def _():
            end_copy(k).start()

    def across(k):
        @pl.when(is_mid)
        def _():
            end_copy(k).wait_recv()
            own_gram[k] = (own_gram[k].astype(f32) + from_end[k].astype(f32)).astype(bf16)
            mid_copy(k).start()

    def back_out(k):
        @pl.when(is_mid)
        def _():
            mid_copy(k).wait_recv()
            gram[k] = (own_gram[k].astype(f32) + from_mid[k].astype(f32)).astype(bf16)
            total_copy(k).start()

    def use(k):
        v, p = chunks[k]

        @pl.when(is_end)
        def _():
            total_copy(k).wait_recv()

        product = jnp.dot(gram[k], norm[1 - v, pl.ds(p * wide, wide)], preferred_element_type=f32)
        if p == 0:
            up[1 - v] = product
        else:
            up[1 - v] += product

    def match(p):
        both = norm[0, pl.ds(p * wide, wide)].astype(f32) * norm[1, pl.ds(p * wide, wide)].astype(f32)
        both = jnp.sum(both, axis=0, keepdims=True)
        diagonal[pl.ds(0, 1)] = both if p == 0 else diagonal[pl.ds(0, 1)] + both

    def back_copy(v, r):
        return remote(back.at[v, 0], back.at[v, r], back_s.at[v, r], back_r.at[v, r], peer(r))

    def upstream(v):
        diag = diagonal[pl.ds(0, 1)] / total_rows
        slope = 2.0 * (diag - 1.0) - 2.0 * OFF_WEIGHT * diag
        mine = norm[v, pl.ds(0, rows)].astype(f32)
        other = norm[1 - v, pl.ds(0, rows)].astype(f32)
        value = up[v] * (2.0 * OFF_WEIGHT / total_rows) + other * slope
        up[v] = value
        back[v, 0, pl.ds(0, 1)] = jnp.sum(value, axis=0, keepdims=True)
        back[v, 0, pl.ds(1, 1)] = jnp.sum(value * mine, axis=0, keepdims=True)
        for r in range(DP - 1, 0, -1):
            back_copy(v, r).start()

    def through_norm(v):
        for r in range(1, DP):
            back_copy(v, r).wait_recv()
        mean_up = sum(back[v, r, pl.ds(0, 1)] for r in range(DP)) / total_rows
        cross = sum(back[v, r, pl.ds(1, 1)] for r in range(DP)) / total_rows
        mine = norm[v, pl.ds(0, rows)].astype(f32)
        delta[v] = (inverse_ref[pl.ds(v, 1)] * (up[v] - mean_up - mine * cross)).astype(bf16)

    slim = width // PARTS

    def outward(v, j, c):
        return remote(
            part.at[v, j, c], from_outer.at[v, j, c], part_s.at[v, j, c], outer_r.at[v, j, c], inner
        )

    def over(v, j, c):
        return remote(
            part.at[v, j, c], from_inner.at[v, 3 - j, c], part_s.at[v, j, c], inner_r.at[v, 3 - j, c], inner
        )

    def homeward(v, c):
        return remote(
            part.at[v, 0, c], from_inner.at[v, 0, c], part_s.at[v, 0, c], inner_r.at[v, 0, c], outer
        )

    def products(v):
        @pl.loop(0, MP * PARTS)
        def _(step):
            j = MP - 1 - lax.div(step, PARTS)
            c = lax.rem(step, PARTS)
            block = jnp.where(low, j, MP - 1 - j)
            start = pl.multiple_of(block * width + c * slim, slim)
            part[v, j, c] = times_t(delta[v], weight[pl.ds(start, slim)]).astype(bf16)

            @pl.when(jnp.logical_and(is_end, j > 0))
            def _():
                outward(v, j, c).start()

    normalize(1, 0)
    got(1, 1)
    normalize(1, 1)
    own(0)
    give_across(1)
    give_own(0)
    got(1, 2, 1)
    give(1, 2, 3, 1)
    got(1, 4, 0)
    give(1, 4, 5, 1)
    normalize(1, 2)
    normalize(1, 4)
    across(0)
    got(1, 3)
    normalize(1, 3)
    own(1)
    got(1, 5)
    normalize(1, 5)
    own(2)
    back_out(0)
    normalize(0, 0)
    got(0, 1)
    normalize(0, 1)
    got(1, 6, 0)
    got(1, 6, 1)
    give(1, 6, 7, 1)
    normalize(1, 6)
    across(1)
    across(2)
    got(1, 7)
    normalize(1, 7)
    own(3)
    own(4)
    back_out(1)
    back_out(2)
    match(0)

    give_across(0)
    use(0)
    across(3)
    across(4)
    got(0, 2, 1)
    give(0, 2, 3, 1)
    got(0, 4, 0)
    give(0, 4, 5, 1)
    normalize(0, 2)
    normalize(0, 4)
    back_out(3)
    back_out(4)
    got(0, 3)
    normalize(0, 3)
    own(5)
    use(1)
    got(0, 5)
    normalize(0, 5)
    own(6)
    use(2)
    match(1)
    match(2)
    across(5)
    across(6)
    got(0, 6, 0)
    got(0, 6, 1)
    give(0, 6, 7, 1)
    normalize(0, 6)
    got(0, 7)
    normalize(0, 7)
    match(3)
    use(3)
    upstream(0)
    own(7)
    back_out(5)
    back_out(6)
    load.wait()
    through_norm(0)
    products(0)

    across(7)
    use(4)
    use(5)
    use(6)
    back_out(7)
    use(7)
    upstream(1)
    through_norm(1)
    products(1)

    outs = (grad_one_ref, grad_two_ref)

    @pl.when(is_end)
    def _():
        for v in range(2):
            for c in range(PARTS):
                homeward(v, c).wait_recv()
                outs[v][:, pl.ds(c * slim, slim)] = (
                    part[v, 0, c].astype(f32) + from_inner[v, 0, c].astype(f32)
                ).astype(bf16)

    @pl.when(is_mid)
    def _():
        def pass_on(v, j, c):
            outward(v, j, c).wait_recv()
            part[v, j, c] = (part[v, j, c].astype(f32) + from_outer[v, j, c].astype(f32)).astype(bf16)
            over(v, j, c).start()

        def pass_home(v, c):
            over(v, 3, c).wait_recv()
            part[v, 0, c] = (part[v, 0, c].astype(f32) + from_inner[v, 0, c].astype(f32)).astype(bf16)
            homeward(v, c).start()

        for v in range(2):
            order = [(3, c) for c in range(PARTS)] + [(2, c) for c in range(PARTS)]
            for at, (j, c) in enumerate(order):
                pass_on(v, j, c)
                if 2 <= at < PARTS + 2:
                    pass_home(v, at - 2)
            for c in range(PARTS):
                over(v, 2, c).wait_recv()
                outward(v, 1, c).wait_recv()
                outs[v][:, pl.ds(c * slim, slim)] = (
                    part[v, 1, c].astype(f32) + from_outer[v, 1, c].astype(f32)
                    + from_inner[v, 1, c].astype(f32)
                ).astype(bf16)

    for r in range(1, DP):
        stat_copy(r).wait_send()
        for v in range(2):
            back_copy(v, r).wait_send()
    for copy in sent:
        copy.wait_send()
    for k in range(len(chunks)):
        end_copy(k).wait_send()

    @pl.when(is_mid)
    def _():
        for k in range(len(chunks)):
            total_copy(k).wait_send()
        for v in range(2):
            for c in range(PARTS):
                for j in (0, 2, 3):
                    outward(v, j, c).wait_send()

    @pl.when(is_end)
    def _():
        for v in range(2):
            for c in range(PARTS):
                for j in (1, 2, 3):
                    outward(v, j, c).wait_send()


def local_fused(view_one, view_two, proj_weight):
    rows, width = view_one.shape
    bf16, f32 = jnp.bfloat16, jnp.float32
    dma = pltpu.SemaphoreType.DMA
    slim = width // PARTS
    out = jax.ShapeDtypeStruct((rows, width), bf16)
    vmem = pl.BlockSpec(memory_space=pltpu.VMEM)
    return pl.pallas_call(
        fused,
        out_shape=(out, out),
        in_specs=[pl.BlockSpec(memory_space=pl.ANY)] * 3,
        out_specs=(vmem, vmem),
        scratch_shapes=[
            pltpu.VMEM(proj_weight.shape, bf16),
            pltpu.VMEM((2, DP * rows, width), bf16),
            pltpu.VMEM((2, DP * rows, width), bf16),
            pltpu.VMEM((DP, 4, width), f32),
            pltpu.VMEM((2, DP, 2, width), f32),
            pltpu.VMEM((8, width), f32),
            pltpu.VMEM((8, width), f32),
            pltpu.VMEM((8, width), f32),
            pltpu.VMEM((2, rows, width), f32),
            pltpu.VMEM((8, rows, 2 * rows), bf16),
            pltpu.VMEM((8, rows, 2 * rows), bf16),
            pltpu.VMEM((8, rows, 2 * rows), bf16),
            pltpu.VMEM((8, rows, 2 * rows), bf16),
            pltpu.VMEM((2, rows, width), bf16),
            pltpu.VMEM((2, MP, PARTS, rows, slim), bf16),
            pltpu.VMEM((2, MP, PARTS, rows, slim), bf16),
            pltpu.VMEM((2, 2, PARTS, rows, slim), bf16),
            dma((2,)),
            dma(()),
            dma((DP,)), dma((DP,)), dma((2, DP)), dma((2, DP)),
            dma((DP, 2, 2)), dma((DP, 2, 2)),
            dma((8,)), dma((8,)), dma((8,)), dma((8,)), dma((8,)),
            dma((2, MP, PARTS)), dma((2, MP, PARTS)), dma((2, 2, PARTS)),
        ],
        compiler_params=pltpu.CompilerParams(
            collective_id=0, has_side_effects=True, vmem_limit_bytes=VMEM_MIB * 1024 * 1024
        ),
        cost_estimate=pl.CostEstimate(
            flops=4 * rows * width * (2 * DP * rows + MP * width),
            bytes_accessed=2 * (MP * width * width + 4 * rows * width),
            transcendentals=0,
        ),
    )(view_one, view_two, proj_weight)


def contract_rows(left, right):
    return lax.dot_general(
        left, right, (((0,), (0,)), ((), ())), preferred_element_type=jnp.float32
    )


def times_transposed(left, right):
    return lax.dot_general(
        left, right, (((1,), (1,)), ((), ())), preferred_element_type=jnp.float32
    )


def local(view_one, view_two, proj_weight):
    row_count, local_width = view_one.shape
    batch_devices = lax.axis_size("dp")
    total_rows = row_count * batch_devices
    first = view_one.astype(jnp.float32)
    second = view_two.astype(jnp.float32)
    sum_one, sum_two = lax.psum((jnp.sum(first, axis=0), jnp.sum(second, axis=0)), "dp")
    center_one = sum_one / total_rows
    center_two = sum_two / total_rows
    centered_one = first - center_one
    centered_two = second - center_two
    square_one, square_two = lax.psum(
        (
            jnp.sum(centered_one * centered_one, axis=0),
            jnp.sum(centered_two * centered_two, axis=0),
        ),
        "dp",
    )
    variance_one = square_one / total_rows
    variance_two = square_two / total_rows
    inverse_one = lax.rsqrt(variance_one + EPSILON)
    inverse_two = lax.rsqrt(variance_two + EPSILON)
    norm_one = (centered_one * inverse_one).astype(jnp.bfloat16)
    norm_two = (centered_two * inverse_two).astype(jnp.bfloat16)
    whole_two = lax.all_gather(norm_two, "mp", axis=1, tiled=True)
    total_width = whole_two.shape[1]
    block_index = lax.axis_index("mp")
    slab_index = lax.axis_index("dp")
    shard_cols = total_width // batch_devices
    corr_part = contract_rows(norm_one, whole_two)
    corr_shard = lax.psum_scatter(corr_part, "dp", scatter_dimension=1, tiled=True) / total_rows
    row_ids = block_index * local_width + lax.broadcasted_iota(
        jnp.int32, (local_width, shard_cols), 0
    )
    col_ids = slab_index * shard_cols + lax.broadcasted_iota(
        jnp.int32, (local_width, shard_cols), 1
    )
    grad_shard = jnp.where(
        row_ids == col_ids, -2.0 * (1.0 - corr_shard), 2.0 * OFF_WEIGHT * corr_shard
    ).astype(jnp.bfloat16)
    piece = lax.all_gather(grad_shard, "dp", axis=1, tiled=True)
    upper = times_transposed(whole_two, piece)
    fresh = jnp.dot(norm_one, piece, preferred_element_type=jnp.float32)
    up_two = lax.psum_scatter(
        fresh.astype(jnp.bfloat16), "mp", scatter_dimension=1, tiled=True
    ).astype(jnp.float32)
    normal_one = norm_one.astype(jnp.float32)
    normal_two = norm_two.astype(jnp.float32)
    mean_up_one, cross_one, mean_up_two, cross_two = lax.psum(
        (
            jnp.sum(upper, axis=0),
            jnp.sum(upper * normal_one, axis=0),
            jnp.sum(up_two, axis=0),
            jnp.sum(up_two * normal_two, axis=0),
        ),
        "dp",
    )
    delta_one = (
        inverse_one * (upper - mean_up_one / total_rows - normal_one * (cross_one / total_rows))
    ).astype(jnp.bfloat16)
    delta_two = (
        inverse_two * (up_two - mean_up_two / total_rows - normal_two * (cross_two / total_rows))
    ).astype(jnp.bfloat16)
    partial_one = times_transposed(delta_one, proj_weight)
    partial_two = times_transposed(delta_two, proj_weight)
    summed_one, summed_two = (
        lax.psum_scatter(
            partial_one.astype(jnp.bfloat16), "mp", scatter_dimension=1, tiled=True
        ).astype(jnp.float32),
        lax.psum_scatter(
            partial_two.astype(jnp.bfloat16), "mp", scatter_dimension=1, tiled=True
        ).astype(jnp.float32),
    )
    return (summed_one.astype(jnp.bfloat16), summed_two.astype(jnp.bfloat16))


def solution(mesh):
    placed = (P("dp", "mp"), P("dp", "mp"), P(None, "mp"))

    def whole(view_one, view_two, proj_weight):
        batch, features = view_one.shape
        suits = dict(mesh.shape) == {"dp": DP, "mp": MP}
        suits = suits and batch % (DP * 128) == 0 and 2 * batch <= features and features <= 4096
        return jax.shard_map(
            local_fused if suits else local,
            mesh=mesh, in_specs=placed, out_specs=(P("dp", "mp"), P("dp", "mp")), check_vma=False,
        )(view_one, view_two, proj_weight)

    return whole
```

```python
import jax
import jax.numpy as jnp
from jax import lax
from jax.experimental import pallas as pl
from jax.experimental.pallas import tpu as pltpu
from jax.sharding import PartitionSpec as P

OFF_WEIGHT = 0.0125
EPSILON = 1e-05
MESH = pl.DeviceIdType.MESH
DP, MP = 8, 4
VMEM_MIB = 48
PARTS = 4


def times_t(left, right):
    return lax.dot_general(
        left, right, (((1,), (1,)), ((), ())), preferred_element_type=jnp.float32
    )


def fused(
    one_hbm, two_hbm, weight_hbm, grad_one_ref, grad_two_ref,
    weight, raw, norm, stat, back, inverse_ref, mean_ref, diagonal, up, own_gram, from_end, from_mid,
    gram, delta, part, from_outer, from_inner,
    view_sem, weight_sem, stat_s, stat_r, back_s, back_r, raw_s, raw_r,
    gram_s, end_r, mid_r, total_s, total_r, part_s, outer_r, inner_r,
):
    rows, width = one_hbm.shape
    total_rows = rows * DP
    half = rows // 2
    bf16, f32 = jnp.bfloat16, jnp.float32
    a, m = lax.axis_index("dp"), lax.axis_index("mp")
    core, along_x, along_y = lax.rem(a, 2), lax.rem(lax.div(a, 2), 2), lax.div(a, 4)

    def peer(r):
        at = a
        if r & 1:
            at = at + 1 - 2 * core
        if r & 2:
            at = at + 2 - 4 * along_x
        if r & 4:
            at = at + 4 - 8 * along_y
        return (at, m)

    low = m < 2
    is_mid = jnp.logical_and(m > 0, m < MP - 1)
    is_end = jnp.logical_not(is_mid)
    inner = (a, jnp.where(low, m + 1, m - 1))
    outer = (a, jnp.where(low, jnp.maximum(m - 1, 0), jnp.minimum(m + 1, MP - 1)))

    def remote(src, dst, send, recv, to):
        return pltpu.make_async_remote_copy(
            src_ref=src, dst_ref=dst, send_sem=send, recv_sem=recv, device_id=to, device_id_type=MESH
        )

    fetch = [
        pltpu.make_async_copy(ref, raw.at[v, pl.ds(0, rows)], view_sem.at[v])
        for v, ref in enumerate((one_hbm, two_hbm))
    ]
    fetch[1].start()
    fetch[0].start()
    load = pltpu.make_async_copy(weight_hbm, weight, weight_sem)
    load.start()

    barrier = pltpu.get_barrier_semaphore()
    for r in range(1, DP):
        pl.semaphore_signal(barrier, inc=1, device_id=peer(r), device_id_type=MESH)
    pl.semaphore_signal(barrier, inc=1, device_id=inner, device_id_type=MESH)

    @pl.when(is_mid)
    def _():
        pl.semaphore_signal(barrier, inc=1, device_id=outer, device_id_type=MESH)

    def raw_copy(v, src, dst, via, h=None):
        size = rows if h is None else half
        skip = 0 if h is None else h * half
        return remote(
            raw.at[v, pl.ds(src * rows + skip, size)], raw.at[v, pl.ds(dst * rows + skip, size)],
            raw_s.at[dst, v, h or 0], raw_r.at[dst, v, h or 0], peer(via),
        )

    def got(v, slot, h=None):
        raw_copy(v, slot, slot, 1, h).wait_recv()

    sent = []

    def give(v, src, dst, via, h=None):
        copy = raw_copy(v, src, dst, via, h)
        copy.start()
        sent.append(copy)

    def give_own(v):
        give(v, 0, 2, 2, 0)
        give(v, 0, 4, 4, 1)
        give(v, 0, 1, 1)
        give(v, 0, 2, 2, 1)
        give(v, 0, 4, 4, 0)

    def give_across(v):
        got(v, 2, 0)
        give(v, 2, 6, 4, 0)
        got(v, 4, 1)
        give(v, 4, 6, 2, 1)

    def block_stat(v):
        x = raw[v, pl.ds(0, rows)].astype(f32)
        mean = jnp.sum(x, axis=0, keepdims=True) / rows
        x = x - mean
        stat[0, pl.ds(2 * v, 1)] = mean
        stat[0, pl.ds(2 * v + 1, 1)] = jnp.sum(x * x, axis=0, keepdims=True)

    def stat_copy(r):
        return remote(stat.at[0], stat.at[r], stat_s.at[r], stat_r.at[r], peer(r))

    for v in (1, 0):
        fetch[v].wait()
        block_stat(v)
    pl.semaphore_wait(barrier, DP + jnp.where(is_mid, 1, 0))
    for r in range(DP - 1, 0, -1):
        stat_copy(r).start()
    give_own(1)
    for r in range(1, DP):
        stat_copy(r).wait_recv()
    for v in range(2):
        means = [stat[r, pl.ds(2 * v, 1)] for r in range(DP)]
        mean = sum(means) / DP
        square = sum(stat[r, pl.ds(2 * v + 1, 1)] for r in range(DP))
        square = square + rows * sum((one - mean) * (one - mean) for one in means)
        mean_ref[pl.ds(v, 1)] = mean
        inverse_ref[pl.ds(v, 1)] = lax.rsqrt(square / total_rows + EPSILON)

    def normalize(v, slot):
        x = raw[v, pl.ds(slot * rows, rows)].astype(f32)
        norm[v, pl.ds(slot * rows, rows)] = (
            (x - mean_ref[pl.ds(v, 1)]) * inverse_ref[pl.ds(v, 1)]
        ).astype(bf16)

    chunks = ((1, 0), (1, 1), (1, 2), (1, 3), (0, 0), (0, 1), (0, 2), (0, 3))
    wide = 2 * rows

    def end_copy(k):
        return remote(own_gram.at[k], from_end.at[k], gram_s.at[k], end_r.at[k], inner)

    def mid_copy(k):
        return remote(own_gram.at[k], from_mid.at[k], gram_s.at[k], mid_r.at[k], inner)

    def total_copy(k):
        return remote(gram.at[k], gram.at[k], total_s.at[k], total_r.at[k], outer)

    def own(k):
        v, p = chunks[k]
        own_gram[k] = times_t(norm[v, pl.ds(0, rows)], norm[v, pl.ds(p * wide, wide)]).astype(bf16)

        @pl.when(is_end)
        def _():
            end_copy(k).start()

    def across(k):
        @pl.when(is_mid)
        def _():
            end_copy(k).wait_recv()
            own_gram[k] = (own_gram[k].astype(f32) + from_end[k].astype(f32)).astype(bf16)
            mid_copy(k).start()

    def back_out(k):
        @pl.when(is_mid)
        def _():
            mid_copy(k).wait_recv()
            gram[k] = (own_gram[k].astype(f32) + from_mid[k].astype(f32)).astype(bf16)
            total_copy(k).start()

    def use(k):
        v, p = chunks[k]

        @pl.when(is_end)
        def _():
            total_copy(k).wait_recv()

        product = jnp.dot(gram[k], norm[1 - v, pl.ds(p * wide, wide)], preferred_element_type=f32)
        if p == 0:
            up[1 - v] = product
        else:
            up[1 - v] += product

    def match(p):
        both = norm[0, pl.ds(p * wide, wide)].astype(f32) * norm[1, pl.ds(p * wide, wide)].astype(f32)
        both = jnp.sum(both, axis=0, keepdims=True)
        diagonal[pl.ds(0, 1)] = both if p == 0 else diagonal[pl.ds(0, 1)] + both

    def back_copy(v, r):
        return remote(back.at[v, 0], back.at[v, r], back_s.at[v, r], back_r.at[v, r], peer(r))

    def upstream(v):
        diag = diagonal[pl.ds(0, 1)] / total_rows
        slope = 2.0 * (diag - 1.0) - 2.0 * OFF_WEIGHT * diag
        mine = norm[v, pl.ds(0, rows)].astype(f32)
        other = norm[1 - v, pl.ds(0, rows)].astype(f32)
        value = up[v] * (2.0 * OFF_WEIGHT / total_rows) + other * slope
        up[v] = value
        back[v, 0, pl.ds(0, 1)] = jnp.sum(value, axis=0, keepdims=True)
        back[v, 0, pl.ds(1, 1)] = jnp.sum(value * mine, axis=0, keepdims=True)
        for r in range(DP - 1, 0, -1):
            back_copy(v, r).start()

    def through_norm(v):
        for r in range(1, DP):
            back_copy(v, r).wait_recv()
        mean_up = sum(back[v, r, pl.ds(0, 1)] for r in range(DP)) / total_rows
        cross = sum(back[v, r, pl.ds(1, 1)] for r in range(DP)) / total_rows
        mine = norm[v, pl.ds(0, rows)].astype(f32)
        delta[v] = (inverse_ref[pl.ds(v, 1)] * (up[v] - mean_up - mine * cross)).astype(bf16)

    slim = width // PARTS

    def outward(v, j, c):
        return remote(
            part.at[v, j, c], from_outer.at[v, j, c], part_s.at[v, j, c], outer_r.at[v, j, c], inner
        )

    def over(v, j, c):
        return remote(
            part.at[v, j, c], from_inner.at[v, 3 - j, c], part_s.at[v, j, c], inner_r.at[v, 3 - j, c], inner
        )

    def homeward(v, c):
        return remote(
            part.at[v, 0, c], from_inner.at[v, 0, c], part_s.at[v, 0, c], inner_r.at[v, 0, c], outer
        )

    def products(v):
        @pl.loop(0, MP * PARTS)
        def _(step):
            j = MP - 1 - lax.div(step, PARTS)
            c = lax.rem(step, PARTS)
            block = jnp.where(low, j, MP - 1 - j)
            start = pl.multiple_of(block * width + c * slim, slim)
            part[v, j, c] = times_t(delta[v], weight[pl.ds(start, slim)]).astype(bf16)

            @pl.when(jnp.logical_and(is_end, j > 0))
            def _():
                outward(v, j, c).start()

    def pass_on(v, j, c):
        outward(v, j, c).wait_recv()
        part[v, j, c] = (part[v, j, c].astype(f32) + from_outer[v, j, c].astype(f32)).astype(bf16)
        over(v, j, c).start()

    def pass_home(v, c):
        over(v, 3, c).wait_recv()
        part[v, 0, c] = (part[v, 0, c].astype(f32) + from_inner[v, 0, c].astype(f32)).astype(bf16)
        homeward(v, c).start()

    normalize(1, 0)
    got(1, 1)
    normalize(1, 1)
    own(0)
    give_across(1)
    give_own(0)
    got(1, 2, 1)
    give(1, 2, 3, 1)
    got(1, 4, 0)
    give(1, 4, 5, 1)
    normalize(1, 2)
    normalize(1, 4)
    across(0)
    got(1, 3)
    normalize(1, 3)
    own(1)
    got(1, 5)
    normalize(1, 5)
    own(2)
    back_out(0)
    normalize(0, 0)
    got(0, 1)
    normalize(0, 1)
    got(1, 6, 0)
    got(1, 6, 1)
    give(1, 6, 7, 1)
    normalize(1, 6)
    across(1)
    across(2)
    got(1, 7)
    normalize(1, 7)
    own(3)
    own(4)
    back_out(1)
    back_out(2)
    match(0)

    give_across(0)
    use(0)
    across(3)
    across(4)
    got(0, 2, 1)
    give(0, 2, 3, 1)
    got(0, 4, 0)
    give(0, 4, 5, 1)
    normalize(0, 2)
    normalize(0, 4)
    back_out(3)
    back_out(4)
    got(0, 3)
    normalize(0, 3)
    own(5)
    use(1)
    got(0, 5)
    normalize(0, 5)
    own(6)
    use(2)
    match(1)
    match(2)
    across(5)
    across(6)
    got(0, 6, 0)
    got(0, 6, 1)
    give(0, 6, 7, 1)
    normalize(0, 6)
    got(0, 7)
    normalize(0, 7)
    match(3)
    use(3)
    upstream(0)
    own(7)
    back_out(5)
    back_out(6)
    load.wait()
    through_norm(0)
    products(0)

    across(7)
    use(4)
    use(5)
    use(6)
    back_out(7)
    use(7)
    upstream(1)

    @pl.when(is_mid)
    def _():
        for c in range(PARTS):
            pass_on(0, MP - 1, c)

    through_norm(1)
    products(1)

    outs = (grad_one_ref, grad_two_ref)

    @pl.when(is_end)
    def _():
        for v in range(2):
            for c in range(PARTS):
                homeward(v, c).wait_recv()
                outs[v][:, pl.ds(c * slim, slim)] = (
                    part[v, 0, c].astype(f32) + from_inner[v, 0, c].astype(f32)
                ).astype(bf16)

    @pl.when(is_mid)
    def _():
        for v in range(2):
            if v == 1:
                for c in range(PARTS):
                    pass_on(v, MP - 1, c)
            for c in range(PARTS):
                pass_home(v, c)
                pass_on(v, MP - 2, c)
            for c in range(PARTS):
                over(v, 2, c).wait_recv()
                outward(v, 1, c).wait_recv()
                outs[v][:, pl.ds(c * slim, slim)] = (
                    part[v, 1, c].astype(f32) + from_outer[v, 1, c].astype(f32)
                    + from_inner[v, 1, c].astype(f32)
                ).astype(bf16)

    for r in range(1, DP):
        stat_copy(r).wait_send()
        for v in range(2):
            back_copy(v, r).wait_send()
    for copy in sent:
        copy.wait_send()
    for k in range(len(chunks)):
        end_copy(k).wait_send()

    @pl.when(is_mid)
    def _():
        for k in range(len(chunks)):
            total_copy(k).wait_send()
        for v in range(2):
            for c in range(PARTS):
                for j in (0, 2, 3):
                    outward(v, j, c).wait_send()

    @pl.when(is_end)
    def _():
        for v in range(2):
            for c in range(PARTS):
                for j in (1, 2, 3):
                    outward(v, j, c).wait_send()


def local_fused(view_one, view_two, proj_weight):
    rows, width = view_one.shape
    bf16, f32 = jnp.bfloat16, jnp.float32
    dma = pltpu.SemaphoreType.DMA
    slim = width // PARTS
    out = jax.ShapeDtypeStruct((rows, width), bf16)
    vmem = pl.BlockSpec(memory_space=pltpu.VMEM)
    return pl.pallas_call(
        fused,
        out_shape=(out, out),
        in_specs=[pl.BlockSpec(memory_space=pltpu.HBM)] * 3,
        out_specs=(vmem, vmem),
        scratch_shapes=[
            pltpu.VMEM(proj_weight.shape, bf16),
            pltpu.VMEM((2, DP * rows, width), bf16),
            pltpu.VMEM((2, DP * rows, width), bf16),
            pltpu.VMEM((DP, 4, width), f32),
            pltpu.VMEM((2, DP, 2, width), f32),
            pltpu.VMEM((8, width), f32),
            pltpu.VMEM((8, width), f32),
            pltpu.VMEM((8, width), f32),
            pltpu.VMEM((2, rows, width), f32),
            pltpu.VMEM((8, rows, 2 * rows), bf16),
            pltpu.VMEM((8, rows, 2 * rows), bf16),
            pltpu.VMEM((8, rows, 2 * rows), bf16),
            pltpu.VMEM((8, rows, 2 * rows), bf16),
            pltpu.VMEM((2, rows, width), bf16),
            pltpu.VMEM((2, MP, PARTS, rows, slim), bf16),
            pltpu.VMEM((2, MP, PARTS, rows, slim), bf16),
            pltpu.VMEM((2, 2, PARTS, rows, slim), bf16),
            dma((2,)),
            dma(()),
            dma((DP,)), dma((DP,)), dma((2, DP)), dma((2, DP)),
            dma((DP, 2, 2)), dma((DP, 2, 2)),
            dma((8,)), dma((8,)), dma((8,)), dma((8,)), dma((8,)),
            dma((2, MP, PARTS)), dma((2, MP, PARTS)), dma((2, 2, PARTS)),
        ],
        compiler_params=pltpu.CompilerParams(
            collective_id=0, has_side_effects=True, vmem_limit_bytes=VMEM_MIB * 1024 * 1024
        ),
        cost_estimate=pl.CostEstimate(
            flops=4 * rows * width * (2 * DP * rows + MP * width),
            bytes_accessed=2 * (MP * width * width + 4 * rows * width),
            transcendentals=0,
        ),
    )(view_one, view_two, proj_weight)


def contract_rows(left, right):
    return lax.dot_general(
        left, right, (((0,), (0,)), ((), ())), preferred_element_type=jnp.float32
    )


def times_transposed(left, right):
    return lax.dot_general(
        left, right, (((1,), (1,)), ((), ())), preferred_element_type=jnp.float32
    )


def local(view_one, view_two, proj_weight):
    row_count, local_width = view_one.shape
    batch_devices = lax.axis_size("dp")
    total_rows = row_count * batch_devices
    first = view_one.astype(jnp.float32)
    second = view_two.astype(jnp.float32)
    sum_one, sum_two = lax.psum((jnp.sum(first, axis=0), jnp.sum(second, axis=0)), "dp")
    center_one = sum_one / total_rows
    center_two = sum_two / total_rows
    centered_one = first - center_one
    centered_two = second - center_two
    square_one, square_two = lax.psum(
        (
            jnp.sum(centered_one * centered_one, axis=0),
            jnp.sum(centered_two * centered_two, axis=0),
        ),
        "dp",
    )
    variance_one = square_one / total_rows
    variance_two = square_two / total_rows
    inverse_one = lax.rsqrt(variance_one + EPSILON)
    inverse_two = lax.rsqrt(variance_two + EPSILON)
    norm_one = (centered_one * inverse_one).astype(jnp.bfloat16)
    norm_two = (centered_two * inverse_two).astype(jnp.bfloat16)
    whole_two = lax.all_gather(norm_two, "mp", axis=1, tiled=True)
    total_width = whole_two.shape[1]
    block_index = lax.axis_index("mp")
    slab_index = lax.axis_index("dp")
    shard_cols = total_width // batch_devices
    corr_part = contract_rows(norm_one, whole_two)
    corr_shard = lax.psum_scatter(corr_part, "dp", scatter_dimension=1, tiled=True) / total_rows
    row_ids = block_index * local_width + lax.broadcasted_iota(
        jnp.int32, (local_width, shard_cols), 0
    )
    col_ids = slab_index * shard_cols + lax.broadcasted_iota(
        jnp.int32, (local_width, shard_cols), 1
    )
    grad_shard = jnp.where(
        row_ids == col_ids, -2.0 * (1.0 - corr_shard), 2.0 * OFF_WEIGHT * corr_shard
    ).astype(jnp.bfloat16)
    piece = lax.all_gather(grad_shard, "dp", axis=1, tiled=True)
    upper = times_transposed(whole_two, piece)
    fresh = jnp.dot(norm_one, piece, preferred_element_type=jnp.float32)
    up_two = lax.psum_scatter(
        fresh.astype(jnp.bfloat16), "mp", scatter_dimension=1, tiled=True
    ).astype(jnp.float32)
    normal_one = norm_one.astype(jnp.float32)
    normal_two = norm_two.astype(jnp.float32)
    mean_up_one, cross_one, mean_up_two, cross_two = lax.psum(
        (
            jnp.sum(upper, axis=0),
            jnp.sum(upper * normal_one, axis=0),
            jnp.sum(up_two, axis=0),
            jnp.sum(up_two * normal_two, axis=0),
        ),
        "dp",
    )
    delta_one = (
        inverse_one * (upper - mean_up_one / total_rows - normal_one * (cross_one / total_rows))
    ).astype(jnp.bfloat16)
    delta_two = (
        inverse_two * (up_two - mean_up_two / total_rows - normal_two * (cross_two / total_rows))
    ).astype(jnp.bfloat16)
    partial_one = times_transposed(delta_one, proj_weight)
    partial_two = times_transposed(delta_two, proj_weight)
    summed_one, summed_two = (
        lax.psum_scatter(
            partial_one.astype(jnp.bfloat16), "mp", scatter_dimension=1, tiled=True
        ).astype(jnp.float32),
        lax.psum_scatter(
            partial_two.astype(jnp.bfloat16), "mp", scatter_dimension=1, tiled=True
        ).astype(jnp.float32),
    )
    return (summed_one.astype(jnp.bfloat16), summed_two.astype(jnp.bfloat16))


def solution(mesh):
    placed = (P("dp", "mp"), P("dp", "mp"), P(None, "mp"))

    def whole(view_one, view_two, proj_weight):
        batch, features = view_one.shape
        suits = dict(mesh.shape) == {"dp": DP, "mp": MP}
        suits = suits and batch % (DP * 128) == 0 and 2 * batch <= features and features <= 4096
        return jax.shard_map(
            local_fused if suits else local,
            mesh=mesh, in_specs=placed, out_specs=(P("dp", "mp"), P("dp", "mp")), check_vma=False,
        )(view_one, view_two, proj_weight)

    return whole
```

```python
import jax
import jax.numpy as jnp
from jax import lax
from jax.experimental import pallas as pl
from jax.experimental.pallas import tpu as pltpu
from jax.sharding import PartitionSpec as P

OFF_WEIGHT = 0.0125
EPSILON = 1e-05
MESH = pl.DeviceIdType.MESH
DP, MP = 8, 4
VMEM_KIB = 54700
PARTS = 4


def times_t(left, right):
    return lax.dot_general(
        left, right, (((1,), (1,)), ((), ())), preferred_element_type=jnp.float32
    )


def fused(
    one_hbm, two_hbm, weight_hbm, grad_one_ref, grad_two_ref,
    weight, raw, norm, stat, back, inverse_ref, mean_ref, diagonal, up, own_gram, from_end, from_mid,
    gram, delta, part, from_outer, from_inner,
    view_sem, weight_sem, stat_s, stat_r, back_s, back_r, raw_s, raw_r,
    gram_s, end_r, mid_r, total_s, total_r, part_s, outer_r, inner_r,
):
    rows, width = one_hbm.shape
    total_rows = rows * DP
    half = rows // 2
    bf16, f32 = jnp.bfloat16, jnp.float32
    a, m = lax.axis_index("dp"), lax.axis_index("mp")
    core, along_x, along_y = lax.rem(a, 2), lax.rem(lax.div(a, 2), 2), lax.div(a, 4)

    def peer(r):
        at = a
        if r & 1:
            at = at + 1 - 2 * core
        if r & 2:
            at = at + 2 - 4 * along_x
        if r & 4:
            at = at + 4 - 8 * along_y
        return (at, m)

    low = m < 2
    is_mid = jnp.logical_and(m > 0, m < MP - 1)
    is_end = jnp.logical_not(is_mid)
    inner = (a, jnp.where(low, m + 1, m - 1))
    outer = (a, jnp.where(low, jnp.maximum(m - 1, 0), jnp.minimum(m + 1, MP - 1)))

    def remote(src, dst, send, recv, to):
        return pltpu.make_async_remote_copy(
            src_ref=src, dst_ref=dst, send_sem=send, recv_sem=recv, device_id=to, device_id_type=MESH
        )

    fetch = [
        pltpu.make_async_copy(ref, raw.at[v, pl.ds(0, rows)], view_sem.at[v])
        for v, ref in enumerate((one_hbm, two_hbm))
    ]
    fetch[1].start()
    fetch[0].start()
    load = pltpu.make_async_copy(weight_hbm, weight, weight_sem)
    load.start()

    barrier = pltpu.get_barrier_semaphore()
    for r in range(1, DP):
        pl.semaphore_signal(barrier, inc=1, device_id=peer(r), device_id_type=MESH)
    pl.semaphore_signal(barrier, inc=1, device_id=inner, device_id_type=MESH)

    @pl.when(is_mid)
    def _():
        pl.semaphore_signal(barrier, inc=1, device_id=outer, device_id_type=MESH)

    def raw_copy(v, src, dst, via, h=None):
        size = rows if h is None else half
        skip = 0 if h is None else h * half
        return remote(
            raw.at[v, pl.ds(src * rows + skip, size)], raw.at[v, pl.ds(dst * rows + skip, size)],
            raw_s.at[dst, v, h or 0], raw_r.at[dst, v, h or 0], peer(via),
        )

    def got(v, slot, h=None):
        raw_copy(v, slot, slot, 1, h).wait_recv()

    sent = []

    def give(v, src, dst, via, h=None):
        copy = raw_copy(v, src, dst, via, h)
        copy.start()
        sent.append(copy)

    def give_own(v):
        give(v, 0, 2, 2, 0)
        give(v, 0, 4, 4, 1)
        give(v, 0, 1, 1)
        give(v, 0, 2, 2, 1)
        give(v, 0, 4, 4, 0)

    def give_across(v):
        got(v, 2, 0)
        give(v, 2, 6, 4, 0)
        got(v, 4, 1)
        give(v, 4, 6, 2, 1)

    def block_stat(v):
        x = raw[v, pl.ds(0, rows)].astype(f32)
        mean = jnp.sum(x, axis=0, keepdims=True) / rows
        x = x - mean
        stat[0, pl.ds(2 * v, 1)] = mean
        stat[0, pl.ds(2 * v + 1, 1)] = jnp.sum(x * x, axis=0, keepdims=True)

    def stat_copy(r):
        return remote(stat.at[0], stat.at[r], stat_s.at[r], stat_r.at[r], peer(r))

    for v in (1, 0):
        fetch[v].wait()
        block_stat(v)
    pl.semaphore_wait(barrier, DP + jnp.where(is_mid, 1, 0))
    for r in range(DP - 1, 0, -1):
        stat_copy(r).start()
    give_own(1)
    for r in range(1, DP):
        stat_copy(r).wait_recv()
    for v in range(2):
        means = [stat[r, pl.ds(2 * v, 1)] for r in range(DP)]
        mean = sum(means) / DP
        square = sum(stat[r, pl.ds(2 * v + 1, 1)] for r in range(DP))
        square = square + rows * sum((one - mean) * (one - mean) for one in means)
        mean_ref[pl.ds(v, 1)] = mean
        inverse_ref[pl.ds(v, 1)] = lax.rsqrt(square / total_rows + EPSILON)

    def normalize(v, slot):
        x = raw[v, pl.ds(slot * rows, rows)].astype(f32)
        norm[v, pl.ds(slot * rows, rows)] = (
            (x - mean_ref[pl.ds(v, 1)]) * inverse_ref[pl.ds(v, 1)]
        ).astype(bf16)

    chunks = ((1, 0), (1, 1), (1, 2), (1, 3), (0, 0), (0, 1), (0, 2), (0, 3))
    wide = 2 * rows

    def end_copy(k):
        return remote(own_gram.at[k], from_end.at[k], gram_s.at[k], end_r.at[k], inner)

    def mid_copy(k):
        return remote(own_gram.at[k], from_mid.at[k], gram_s.at[k], mid_r.at[k], inner)

    def total_copy(k):
        return remote(gram.at[k], gram.at[k], total_s.at[k], total_r.at[k], outer)

    def own(k):
        v, p = chunks[k]
        own_gram[k] = times_t(norm[v, pl.ds(0, rows)], norm[v, pl.ds(p * wide, wide)]).astype(bf16)

        @pl.when(is_end)
        def _():
            end_copy(k).start()

    def across(k):
        @pl.when(is_mid)
        def _():
            end_copy(k).wait_recv()
            own_gram[k] = (own_gram[k].astype(f32) + from_end[k].astype(f32)).astype(bf16)
            mid_copy(k).start()

    def back_out(k):
        @pl.when(is_mid)
        def _():
            mid_copy(k).wait_recv()
            gram[k] = (own_gram[k].astype(f32) + from_mid[k].astype(f32)).astype(bf16)
            total_copy(k).start()

    def use(k):
        v, p = chunks[k]

        @pl.when(is_end)
        def _():
            total_copy(k).wait_recv()

        product = jnp.dot(gram[k], norm[1 - v, pl.ds(p * wide, wide)], preferred_element_type=f32)
        if p == 0:
            up[1 - v] = product
        else:
            up[1 - v] += product

    def match(p):
        both = norm[0, pl.ds(p * wide, wide)].astype(f32) * norm[1, pl.ds(p * wide, wide)].astype(f32)
        both = jnp.sum(both, axis=0, keepdims=True)
        diagonal[pl.ds(0, 1)] = both if p == 0 else diagonal[pl.ds(0, 1)] + both

    def back_copy(v, r):
        return remote(back.at[v, 0], back.at[v, r], back_s.at[v, r], back_r.at[v, r], peer(r))

    def upstream(v):
        diag = diagonal[pl.ds(0, 1)] / total_rows
        slope = 2.0 * (diag - 1.0) - 2.0 * OFF_WEIGHT * diag
        mine = norm[v, pl.ds(0, rows)].astype(f32)
        other = norm[1 - v, pl.ds(0, rows)].astype(f32)
        value = up[v] * (2.0 * OFF_WEIGHT / total_rows) + other * slope
        up[v] = value
        back[v, 0, pl.ds(0, 1)] = jnp.sum(value, axis=0, keepdims=True)
        back[v, 0, pl.ds(1, 1)] = jnp.sum(value * mine, axis=0, keepdims=True)
        for r in range(DP - 1, 0, -1):
            back_copy(v, r).start()

    def through_norm(v):
        for r in range(1, DP):
            back_copy(v, r).wait_recv()
        mean_up = sum(back[v, r, pl.ds(0, 1)] for r in range(DP)) / total_rows
        cross = sum(back[v, r, pl.ds(1, 1)] for r in range(DP)) / total_rows
        mine = norm[v, pl.ds(0, rows)].astype(f32)
        delta[v] = (inverse_ref[pl.ds(v, 1)] * (up[v] - mean_up - mine * cross)).astype(bf16)

    slim = width // PARTS

    def outward(v, j, c):
        return remote(
            part.at[v, j, c], from_outer.at[v, j, c], part_s.at[v, j, c], outer_r.at[v, j, c], inner
        )

    def over(v, j, c):
        return remote(
            part.at[v, j, c], from_inner.at[v, 3 - j, c], part_s.at[v, j, c], inner_r.at[v, 3 - j, c], inner
        )

    def homeward(v, c):
        return remote(
            part.at[v, 0, c], from_inner.at[v, 0, c], part_s.at[v, 0, c], inner_r.at[v, 0, c], outer
        )

    def products(v):
        @pl.loop(0, MP * PARTS)
        def _(step):
            j = MP - 1 - lax.div(step, PARTS)
            c = lax.rem(step, PARTS)
            block = jnp.where(low, j, MP - 1 - j)
            start = pl.multiple_of(block * width + c * slim, slim)
            part[v, j, c] = times_t(delta[v], weight[pl.ds(start, slim)]).astype(bf16)

            @pl.when(jnp.logical_and(is_end, j > 0))
            def _():
                outward(v, j, c).start()

    def pass_on(v, j, c):
        outward(v, j, c).wait_recv()
        part[v, j, c] = (part[v, j, c].astype(f32) + from_outer[v, j, c].astype(f32)).astype(bf16)
        over(v, j, c).start()

    def pass_home(v, c):
        over(v, 3, c).wait_recv()
        part[v, 0, c] = (part[v, 0, c].astype(f32) + from_inner[v, 0, c].astype(f32)).astype(bf16)
        homeward(v, c).start()

    normalize(1, 0)
    got(1, 1)
    normalize(1, 1)
    own(0)
    give_across(1)
    give_own(0)
    got(1, 2, 1)
    give(1, 2, 3, 1)
    got(1, 4, 0)
    give(1, 4, 5, 1)
    normalize(1, 2)
    normalize(1, 4)
    across(0)
    got(1, 3)
    normalize(1, 3)
    own(1)
    got(1, 5)
    normalize(1, 5)
    own(2)
    back_out(0)
    normalize(0, 0)
    got(0, 1)
    normalize(0, 1)
    got(1, 6, 0)
    got(1, 6, 1)
    give(1, 6, 7, 1)
    normalize(1, 6)
    across(1)
    across(2)
    got(1, 7)
    normalize(1, 7)
    own(3)
    own(4)
    back_out(1)
    back_out(2)
    match(0)

    give_across(0)
    use(0)
    across(3)
    across(4)
    got(0, 2, 1)
    give(0, 2, 3, 1)
    got(0, 4, 0)
    give(0, 4, 5, 1)
    normalize(0, 2)
    normalize(0, 4)
    back_out(3)
    back_out(4)
    got(0, 3)
    normalize(0, 3)
    own(5)
    use(1)
    got(0, 5)
    normalize(0, 5)
    own(6)
    use(2)
    match(1)
    match(2)
    across(5)
    across(6)
    got(0, 6, 0)
    give(0, 6, 7, 1, 0)
    got(0, 6, 1)
    give(0, 6, 7, 1, 1)
    normalize(0, 6)
    got(0, 7, 0)
    got(0, 7, 1)
    normalize(0, 7)
    match(3)
    use(3)
    upstream(0)
    own(7)
    back_out(5)
    back_out(6)
    use(4)
    load.wait()
    through_norm(0)
    across(7)
    products(0)

    back_out(7)
    use(5)
    use(6)
    use(7)
    upstream(1)

    @pl.when(is_mid)
    def _():
        for c in range(PARTS):
            pass_on(0, MP - 1, c)

    through_norm(1)
    products(1)

    outs = (grad_one_ref, grad_two_ref)

    @pl.when(is_end)
    def _():
        for v in range(2):
            for c in range(PARTS):
                homeward(v, c).wait_recv()
                outs[v][:, pl.ds(c * slim, slim)] = (
                    part[v, 0, c].astype(f32) + from_inner[v, 0, c].astype(f32)
                ).astype(bf16)

    @pl.when(is_mid)
    def _():
        for v in range(2):
            if v == 1:
                for c in range(PARTS):
                    pass_on(v, MP - 1, c)
            for c in range(PARTS):
                pass_home(v, c)
                pass_on(v, MP - 2, c)
            for c in range(PARTS):
                over(v, 2, c).wait_recv()
                outward(v, 1, c).wait_recv()
                outs[v][:, pl.ds(c * slim, slim)] = (
                    part[v, 1, c].astype(f32) + from_outer[v, 1, c].astype(f32)
                    + from_inner[v, 1, c].astype(f32)
                ).astype(bf16)

    for r in range(1, DP):
        stat_copy(r).wait_send()
        for v in range(2):
            back_copy(v, r).wait_send()
    for copy in sent:
        copy.wait_send()
    for k in range(len(chunks)):
        end_copy(k).wait_send()

    @pl.when(is_mid)
    def _():
        for k in range(len(chunks)):
            total_copy(k).wait_send()
        for v in range(2):
            for c in range(PARTS):
                for j in (0, 2, 3):
                    outward(v, j, c).wait_send()

    @pl.when(is_end)
    def _():
        for v in range(2):
            for c in range(PARTS):
                for j in (1, 2, 3):
                    outward(v, j, c).wait_send()


def local_fused(view_one, view_two, proj_weight):
    rows, width = view_one.shape
    bf16, f32 = jnp.bfloat16, jnp.float32
    dma = pltpu.SemaphoreType.DMA
    slim = width // PARTS
    out = jax.ShapeDtypeStruct((rows, width), bf16)
    vmem = pl.BlockSpec(memory_space=pltpu.VMEM)
    return pl.pallas_call(
        fused,
        out_shape=(out, out),
        in_specs=[pl.BlockSpec(memory_space=pltpu.HBM)] * 3,
        out_specs=(vmem, vmem),
        scratch_shapes=[
            pltpu.VMEM(proj_weight.shape, bf16),
            pltpu.VMEM((2, DP * rows, width), bf16),
            pltpu.VMEM((2, DP * rows, width), bf16),
            pltpu.VMEM((DP, 4, width), f32),
            pltpu.VMEM((2, DP, 2, width), f32),
            pltpu.VMEM((8, width), f32),
            pltpu.VMEM((8, width), f32),
            pltpu.VMEM((8, width), f32),
            pltpu.VMEM((2, rows, width), f32),
            pltpu.VMEM((8, rows, 2 * rows), bf16),
            pltpu.VMEM((8, rows, 2 * rows), bf16),
            pltpu.VMEM((8, rows, 2 * rows), bf16),
            pltpu.VMEM((8, rows, 2 * rows), bf16),
            pltpu.VMEM((2, rows, width), bf16),
            pltpu.VMEM((2, MP, PARTS, rows, slim), bf16),
            pltpu.VMEM((2, MP, PARTS, rows, slim), bf16),
            pltpu.VMEM((2, 2, PARTS, rows, slim), bf16),
            dma((2,)),
            dma(()),
            dma((DP,)), dma((DP,)), dma((2, DP)), dma((2, DP)),
            dma((DP, 2, 2)), dma((DP, 2, 2)),
            dma((8,)), dma((8,)), dma((8,)), dma((8,)), dma((8,)),
            dma((2, MP, PARTS)), dma((2, MP, PARTS)), dma((2, 2, PARTS)),
        ],
        compiler_params=pltpu.CompilerParams(
            collective_id=0, has_side_effects=True, vmem_limit_bytes=VMEM_KIB * 1024
        ),
        cost_estimate=pl.CostEstimate(
            flops=4 * rows * width * (2 * DP * rows + MP * width),
            bytes_accessed=2 * (MP * width * width + 4 * rows * width),
            transcendentals=0,
        ),
    )(view_one, view_two, proj_weight)


def contract_rows(left, right):
    return lax.dot_general(
        left, right, (((0,), (0,)), ((), ())), preferred_element_type=jnp.float32
    )


def times_transposed(left, right):
    return lax.dot_general(
        left, right, (((1,), (1,)), ((), ())), preferred_element_type=jnp.float32
    )


def local(view_one, view_two, proj_weight):
    row_count, local_width = view_one.shape
    batch_devices = lax.axis_size("dp")
    total_rows = row_count * batch_devices
    first = view_one.astype(jnp.float32)
    second = view_two.astype(jnp.float32)
    sum_one, sum_two = lax.psum((jnp.sum(first, axis=0), jnp.sum(second, axis=0)), "dp")
    center_one = sum_one / total_rows
    center_two = sum_two / total_rows
    centered_one = first - center_one
    centered_two = second - center_two
    square_one, square_two = lax.psum(
        (
            jnp.sum(centered_one * centered_one, axis=0),
            jnp.sum(centered_two * centered_two, axis=0),
        ),
        "dp",
    )
    variance_one = square_one / total_rows
    variance_two = square_two / total_rows
    inverse_one = lax.rsqrt(variance_one + EPSILON)
    inverse_two = lax.rsqrt(variance_two + EPSILON)
    norm_one = (centered_one * inverse_one).astype(jnp.bfloat16)
    norm_two = (centered_two * inverse_two).astype(jnp.bfloat16)
    whole_two = lax.all_gather(norm_two, "mp", axis=1, tiled=True)
    total_width = whole_two.shape[1]
    block_index = lax.axis_index("mp")
    slab_index = lax.axis_index("dp")
    shard_cols = total_width // batch_devices
    corr_part = contract_rows(norm_one, whole_two)
    corr_shard = lax.psum_scatter(corr_part, "dp", scatter_dimension=1, tiled=True) / total_rows
    row_ids = block_index * local_width + lax.broadcasted_iota(
        jnp.int32, (local_width, shard_cols), 0
    )
    col_ids = slab_index * shard_cols + lax.broadcasted_iota(
        jnp.int32, (local_width, shard_cols), 1
    )
    grad_shard = jnp.where(
        row_ids == col_ids, -2.0 * (1.0 - corr_shard), 2.0 * OFF_WEIGHT * corr_shard
    ).astype(jnp.bfloat16)
    piece = lax.all_gather(grad_shard, "dp", axis=1, tiled=True)
    upper = times_transposed(whole_two, piece)
    fresh = jnp.dot(norm_one, piece, preferred_element_type=jnp.float32)
    up_two = lax.psum_scatter(
        fresh.astype(jnp.bfloat16), "mp", scatter_dimension=1, tiled=True
    ).astype(jnp.float32)
    normal_one = norm_one.astype(jnp.float32)
    normal_two = norm_two.astype(jnp.float32)
    mean_up_one, cross_one, mean_up_two, cross_two = lax.psum(
        (
            jnp.sum(upper, axis=0),
            jnp.sum(upper * normal_one, axis=0),
            jnp.sum(up_two, axis=0),
            jnp.sum(up_two * normal_two, axis=0),
        ),
        "dp",
    )
    delta_one = (
        inverse_one * (upper - mean_up_one / total_rows - normal_one * (cross_one / total_rows))
    ).astype(jnp.bfloat16)
    delta_two = (
        inverse_two * (up_two - mean_up_two / total_rows - normal_two * (cross_two / total_rows))
    ).astype(jnp.bfloat16)
    partial_one = times_transposed(delta_one, proj_weight)
    partial_two = times_transposed(delta_two, proj_weight)
    summed_one, summed_two = (
        lax.psum_scatter(
            partial_one.astype(jnp.bfloat16), "mp", scatter_dimension=1, tiled=True
        ).astype(jnp.float32),
        lax.psum_scatter(
            partial_two.astype(jnp.bfloat16), "mp", scatter_dimension=1, tiled=True
        ).astype(jnp.float32),
    )
    return (summed_one.astype(jnp.bfloat16), summed_two.astype(jnp.bfloat16))


def solution(mesh):
    placed = (P("dp", "mp"), P("dp", "mp"), P(None, "mp"))

    def whole(view_one, view_two, proj_weight):
        batch, features = view_one.shape
        suits = dict(mesh.shape) == {"dp": DP, "mp": MP}
        suits = suits and batch % (DP * 128) == 0 and 2 * batch <= features and features <= 4096
        return jax.shard_map(
            local_fused if suits else local,
            mesh=mesh, in_specs=placed, out_specs=(P("dp", "mp"), P("dp", "mp")), check_vma=False,
        )(view_one, view_two, proj_weight)

    return whole
```

```python
import jax
import jax.numpy as jnp
from jax import lax
from jax.experimental import pallas as pl
from jax.experimental.pallas import tpu as pltpu
from jax.sharding import PartitionSpec as P

OFF_WEIGHT = 0.0125
EPSILON = 1e-05
MESH = pl.DeviceIdType.MESH
DP, MP = 8, 4
VMEM_KIB = 54700
PARTS = 4


def times_t(left, right):
    return lax.dot_general(
        left, right, (((1,), (1,)), ((), ())), preferred_element_type=jnp.float32
    )


def fused(
    one_hbm, two_hbm, weight_hbm, grad_one_ref, grad_two_ref,
    weight, raw, norm, stat, back, inverse_ref, mean_ref, diagonal, up, own_gram, from_end, from_mid,
    gram, delta, part, from_outer, from_inner,
    view_sem, weight_sem, stat_s, stat_r, back_s, back_r, raw_s, raw_r,
    gram_s, end_r, mid_r, total_s, total_r, part_s, outer_r, inner_r,
):
    rows, width = one_hbm.shape
    total_rows = rows * DP
    half = rows // 2
    bf16, f32 = jnp.bfloat16, jnp.float32
    a, m = lax.axis_index("dp"), lax.axis_index("mp")
    core, along_x, along_y = lax.rem(a, 2), lax.rem(lax.div(a, 2), 2), lax.div(a, 4)

    def peer(r):
        at = a
        if r & 1:
            at = at + 1 - 2 * core
        if r & 2:
            at = at + 2 - 4 * along_x
        if r & 4:
            at = at + 4 - 8 * along_y
        return (at, m)

    low = m < 2
    is_mid = jnp.logical_and(m > 0, m < MP - 1)
    is_end = jnp.logical_not(is_mid)
    inner = (a, jnp.where(low, m + 1, m - 1))
    outer = (a, jnp.where(low, jnp.maximum(m - 1, 0), jnp.minimum(m + 1, MP - 1)))

    def remote(src, dst, send, recv, to):
        return pltpu.make_async_remote_copy(
            src_ref=src, dst_ref=dst, send_sem=send, recv_sem=recv, device_id=to, device_id_type=MESH
        )

    fetch = [
        pltpu.make_async_copy(ref, raw.at[v, pl.ds(0, rows)], view_sem.at[v])
        for v, ref in enumerate((one_hbm, two_hbm))
    ]
    fetch[1].start()
    fetch[0].start()
    load = pltpu.make_async_copy(weight_hbm, weight, weight_sem)
    load.start()

    barrier = pltpu.get_barrier_semaphore()
    for r in range(1, DP):
        pl.semaphore_signal(barrier, inc=1, device_id=peer(r), device_id_type=MESH)
    pl.semaphore_signal(barrier, inc=1, device_id=inner, device_id_type=MESH)

    @pl.when(is_mid)
    def _():
        pl.semaphore_signal(barrier, inc=1, device_id=outer, device_id_type=MESH)

    def raw_copy(v, src, dst, via, h=None):
        size = rows if h is None else half
        skip = 0 if h is None else h * half
        return remote(
            raw.at[v, pl.ds(src * rows + skip, size)], raw.at[v, pl.ds(dst * rows + skip, size)],
            raw_s.at[dst, v, h or 0], raw_r.at[dst, v, h or 0], peer(via),
        )

    def got(v, slot, h=None):
        raw_copy(v, slot, slot, 1, h).wait_recv()

    sent = []

    def give(v, src, dst, via, h=None):
        copy = raw_copy(v, src, dst, via, h)
        copy.start()
        sent.append(copy)

    def give_own(v):
        give(v, 0, 2, 2, 0)
        give(v, 0, 4, 4, 1)
        give(v, 0, 1, 1)
        give(v, 0, 2, 2, 1)
        give(v, 0, 4, 4, 0)

    def give_across(v):
        got(v, 2, 0)
        give(v, 2, 6, 4, 0)
        got(v, 4, 1)
        give(v, 4, 6, 2, 1)

    def block_stat(v):
        x = raw[v, pl.ds(0, rows)].astype(f32)
        mean = jnp.sum(x, axis=0, keepdims=True) / rows
        x = x - mean
        stat[0, pl.ds(2 * v, 1)] = mean
        stat[0, pl.ds(2 * v + 1, 1)] = jnp.sum(x * x, axis=0, keepdims=True)

    def stat_copy(r):
        return remote(stat.at[0], stat.at[r], stat_s.at[r], stat_r.at[r], peer(r))

    for v in (1, 0):
        fetch[v].wait()
        block_stat(v)
    pl.semaphore_wait(barrier, DP + jnp.where(is_mid, 1, 0))
    for r in range(DP - 1, 0, -1):
        stat_copy(r).start()
    give_own(1)
    for r in range(1, DP):
        stat_copy(r).wait_recv()
    for v in range(2):
        means = [stat[r, pl.ds(2 * v, 1)] for r in range(DP)]
        mean = sum(means) / DP
        square = sum(stat[r, pl.ds(2 * v + 1, 1)] for r in range(DP))
        square = square + rows * sum((one - mean) * (one - mean) for one in means)
        mean_ref[pl.ds(v, 1)] = mean
        inverse_ref[pl.ds(v, 1)] = lax.rsqrt(square / total_rows + EPSILON)

    def normalize(v, slot):
        x = raw[v, pl.ds(slot * rows, rows)].astype(f32)
        norm[v, pl.ds(slot * rows, rows)] = (
            (x - mean_ref[pl.ds(v, 1)]) * inverse_ref[pl.ds(v, 1)]
        ).astype(bf16)

    chunks = ((1, 0), (1, 1), (1, 2), (1, 3), (0, 0), (0, 1), (0, 2), (0, 3))
    wide = 2 * rows

    def end_copy(k):
        return remote(own_gram.at[k], from_end.at[k], gram_s.at[k], end_r.at[k], inner)

    def mid_copy(k):
        return remote(own_gram.at[k], from_mid.at[k], gram_s.at[k], mid_r.at[k], inner)

    def total_copy(k):
        return remote(gram.at[k], gram.at[k], total_s.at[k], total_r.at[k], outer)

    def own(k):
        v, p = chunks[k]
        own_gram[k] = times_t(norm[v, pl.ds(0, rows)], norm[v, pl.ds(p * wide, wide)]).astype(bf16)

        @pl.when(is_end)
        def _():
            end_copy(k).start()

    def across(k):
        @pl.when(is_mid)
        def _():
            end_copy(k).wait_recv()
            own_gram[k] = (own_gram[k].astype(f32) + from_end[k].astype(f32)).astype(bf16)
            mid_copy(k).start()

    def back_out(k):
        @pl.when(is_mid)
        def _():
            mid_copy(k).wait_recv()
            gram[k] = (own_gram[k].astype(f32) + from_mid[k].astype(f32)).astype(bf16)
            total_copy(k).start()

    def use(k, slots=(0, 1)):
        v, p = chunks[k]

        if slots[0] == 0:
            @pl.when(is_end)
            def _():
                total_copy(k).wait_recv()

        skip, size = slots[0] * rows, len(slots) * rows
        product = jnp.dot(
            gram[k, :, pl.ds(skip, size)], norm[1 - v, pl.ds(p * wide + skip, size)],
            preferred_element_type=f32,
        )
        if p == 0:
            up[1 - v] = product
        else:
            up[1 - v] += product

    def match(p, slots=(0, 1)):
        at = pl.ds(p * wide + slots[0] * rows, len(slots) * rows)
        both = norm[0, at].astype(f32) * norm[1, at].astype(f32)
        both = jnp.sum(both, axis=0, keepdims=True)
        diagonal[pl.ds(0, 1)] = both if p == 0 else diagonal[pl.ds(0, 1)] + both

    def back_copy(v, r):
        return remote(back.at[v, 0], back.at[v, r], back_s.at[v, r], back_r.at[v, r], peer(r))

    def upstream(v):
        diag = diagonal[pl.ds(0, 1)] / total_rows
        slope = 2.0 * (diag - 1.0) - 2.0 * OFF_WEIGHT * diag
        mine = norm[v, pl.ds(0, rows)].astype(f32)
        other = norm[1 - v, pl.ds(0, rows)].astype(f32)
        value = up[v] * (2.0 * OFF_WEIGHT / total_rows) + other * slope
        up[v] = value
        back[v, 0, pl.ds(0, 1)] = jnp.sum(value, axis=0, keepdims=True)
        back[v, 0, pl.ds(1, 1)] = jnp.sum(value * mine, axis=0, keepdims=True)
        for r in range(DP - 1, 0, -1):
            back_copy(v, r).start()

    def through_norm(v):
        for r in range(1, DP):
            back_copy(v, r).wait_recv()
        mean_up = sum(back[v, r, pl.ds(0, 1)] for r in range(DP)) / total_rows
        cross = sum(back[v, r, pl.ds(1, 1)] for r in range(DP)) / total_rows
        mine = norm[v, pl.ds(0, rows)].astype(f32)
        delta[v] = (inverse_ref[pl.ds(v, 1)] * (up[v] - mean_up - mine * cross)).astype(bf16)

    slim = width // PARTS

    def outward(v, j, c):
        return remote(
            part.at[v, j, c], from_outer.at[v, j, c], part_s.at[v, j, c], outer_r.at[v, j, c], inner
        )

    def over(v, j, c):
        return remote(
            part.at[v, j, c], from_inner.at[v, 3 - j, c], part_s.at[v, j, c], inner_r.at[v, 3 - j, c], inner
        )

    def homeward(v, c):
        return remote(
            part.at[v, 0, c], from_inner.at[v, 0, c], part_s.at[v, 0, c], inner_r.at[v, 0, c], outer
        )

    def products(v):
        @pl.loop(0, MP * PARTS)
        def _(step):
            j = MP - 1 - lax.div(step, PARTS)
            c = lax.rem(step, PARTS)
            block = jnp.where(low, j, MP - 1 - j)
            start = pl.multiple_of(block * width + c * slim, slim)
            part[v, j, c] = times_t(delta[v], weight[pl.ds(start, slim)]).astype(bf16)

            @pl.when(jnp.logical_and(is_end, j > 0))
            def _():
                outward(v, j, c).start()

    def pass_on(v, j, c):
        outward(v, j, c).wait_recv()
        part[v, j, c] = (part[v, j, c].astype(f32) + from_outer[v, j, c].astype(f32)).astype(bf16)
        over(v, j, c).start()

    def pass_home(v, c):
        over(v, 3, c).wait_recv()
        part[v, 0, c] = (part[v, 0, c].astype(f32) + from_inner[v, 0, c].astype(f32)).astype(bf16)
        homeward(v, c).start()

    normalize(1, 0)
    got(1, 1)
    normalize(1, 1)
    own(0)
    give_across(1)
    give_own(0)
    got(1, 2, 1)
    give(1, 2, 3, 1)
    got(1, 4, 0)
    give(1, 4, 5, 1)
    normalize(1, 2)
    normalize(1, 4)
    across(0)
    got(1, 3)
    normalize(1, 3)
    own(1)
    got(1, 5)
    normalize(1, 5)
    own(2)
    back_out(0)
    normalize(0, 0)
    got(0, 1)
    normalize(0, 1)
    got(1, 6, 0)
    got(1, 6, 1)
    give(1, 6, 7, 1)
    normalize(1, 6)
    across(1)
    across(2)
    got(1, 7)
    normalize(1, 7)
    own(3)
    own(4)
    match(0)

    give_across(0)
    back_out(1)
    back_out(2)
    use(0)
    across(3)
    across(4)
    got(0, 2, 1)
    give(0, 2, 3, 1)
    got(0, 4, 0)
    give(0, 4, 5, 1)
    normalize(0, 2)
    normalize(0, 4)
    got(0, 3)
    normalize(0, 3)
    own(5)
    back_out(3)
    use(1)
    got(0, 5)
    normalize(0, 5)
    own(6)
    back_out(4)
    use(2)
    match(1)
    match(2)
    across(5)
    across(6)
    got(0, 6, 0)
    give(0, 6, 7, 1, 0)
    got(0, 6, 1)
    give(0, 6, 7, 1, 1)
    normalize(0, 6)
    match(3, (0,))
    use(3, (0,))
    got(0, 7, 0)
    got(0, 7, 1)
    normalize(0, 7)
    match(3, (1,))
    use(3, (1,))
    upstream(0)
    own(7)
    back_out(5)
    back_out(6)
    use(4)
    load.wait()
    through_norm(0)
    across(7)
    products(0)

    back_out(7)
    use(5)
    use(6)
    use(7)
    upstream(1)

    @pl.when(is_mid)
    def _():
        for c in range(PARTS):
            pass_on(0, MP - 1, c)

    through_norm(1)
    products(1)

    outs = (grad_one_ref, grad_two_ref)

    def all_left():
        for r in range(1, DP):
            stat_copy(r).wait_send()
            for v in range(2):
                back_copy(v, r).wait_send()
        for copy in sent:
            copy.wait_send()
        for k in range(len(chunks)):
            end_copy(k).wait_send()

    def parts_left(v, blocks):
        for j in blocks:
            for c in range(PARTS):
                outward(v, j, c).wait_send()

    @pl.when(is_end)
    def _():
        all_left()
        for v in range(2):
            for c in range(PARTS):
                homeward(v, c).wait_recv()
                outs[v][:, pl.ds(c * slim, slim)] = (
                    part[v, 0, c].astype(f32) + from_inner[v, 0, c].astype(f32)
                ).astype(bf16)
            parts_left(v, (3, 2, 1))

    @pl.when(is_mid)
    def _():
        for v in range(2):
            if v == 1:
                for c in range(PARTS):
                    pass_on(v, MP - 1, c)
            for c in range(PARTS):
                pass_home(v, c)
                pass_on(v, MP - 2, c)
            if v == 0:
                all_left()
                for k in range(len(chunks)):
                    total_copy(k).wait_send()
            parts_left(v, (3, 0))
            for c in range(PARTS):
                over(v, 2, c).wait_recv()
                outward(v, 1, c).wait_recv()
                outs[v][:, pl.ds(c * slim, slim)] = (
                    part[v, 1, c].astype(f32) + from_outer[v, 1, c].astype(f32)
                    + from_inner[v, 1, c].astype(f32)
                ).astype(bf16)
            parts_left(v, (2,))


def local_fused(view_one, view_two, proj_weight):
    rows, width = view_one.shape
    bf16, f32 = jnp.bfloat16, jnp.float32
    dma = pltpu.SemaphoreType.DMA
    slim = width // PARTS
    out = jax.ShapeDtypeStruct((rows, width), bf16)
    vmem = pl.BlockSpec(memory_space=pltpu.VMEM)
    return pl.pallas_call(
        fused,
        out_shape=(out, out),
        in_specs=[pl.BlockSpec(memory_space=pltpu.HBM)] * 3,
        out_specs=(vmem, vmem),
        scratch_shapes=[
            pltpu.VMEM(proj_weight.shape, bf16),
            pltpu.VMEM((2, DP * rows, width), bf16),
            pltpu.VMEM((2, DP * rows, width), bf16),
            pltpu.VMEM((DP, 4, width), f32),
            pltpu.VMEM((2, DP, 2, width), f32),
            pltpu.VMEM((8, width), f32),
            pltpu.VMEM((8, width), f32),
            pltpu.VMEM((8, width), f32),
            pltpu.VMEM((2, rows, width), f32),
            pltpu.VMEM((8, rows, 2 * rows), bf16),
            pltpu.VMEM((8, rows, 2 * rows), bf16),
            pltpu.VMEM((8, rows, 2 * rows), bf16),
            pltpu.VMEM((8, rows, 2 * rows), bf16),
            pltpu.VMEM((2, rows, width), bf16),
            pltpu.VMEM((2, MP, PARTS, rows, slim), bf16),
            pltpu.VMEM((2, MP, PARTS, rows, slim), bf16),
            pltpu.VMEM((2, 2, PARTS, rows, slim), bf16),
            dma((2,)),
            dma(()),
            dma((DP,)), dma((DP,)), dma((2, DP)), dma((2, DP)),
            dma((DP, 2, 2)), dma((DP, 2, 2)),
            dma((8,)), dma((8,)), dma((8,)), dma((8,)), dma((8,)),
            dma((2, MP, PARTS)), dma((2, MP, PARTS)), dma((2, 2, PARTS)),
        ],
        compiler_params=pltpu.CompilerParams(
            collective_id=0, has_side_effects=True, vmem_limit_bytes=VMEM_KIB * 1024
        ),
        cost_estimate=pl.CostEstimate(
            flops=4 * rows * width * (2 * DP * rows + MP * width),
            bytes_accessed=2 * (MP * width * width + 4 * rows * width),
            transcendentals=0,
        ),
    )(view_one, view_two, proj_weight)


def contract_rows(left, right):
    return lax.dot_general(
        left, right, (((0,), (0,)), ((), ())), preferred_element_type=jnp.float32
    )


def times_transposed(left, right):
    return lax.dot_general(
        left, right, (((1,), (1,)), ((), ())), preferred_element_type=jnp.float32
    )


def local(view_one, view_two, proj_weight):
    row_count, local_width = view_one.shape
    batch_devices = lax.axis_size("dp")
    total_rows = row_count * batch_devices
    first = view_one.astype(jnp.float32)
    second = view_two.astype(jnp.float32)
    sum_one, sum_two = lax.psum((jnp.sum(first, axis=0), jnp.sum(second, axis=0)), "dp")
    center_one = sum_one / total_rows
    center_two = sum_two / total_rows
    centered_one = first - center_one
    centered_two = second - center_two
    square_one, square_two = lax.psum(
        (
            jnp.sum(centered_one * centered_one, axis=0),
            jnp.sum(centered_two * centered_two, axis=0),
        ),
        "dp",
    )
    variance_one = square_one / total_rows
    variance_two = square_two / total_rows
    inverse_one = lax.rsqrt(variance_one + EPSILON)
    inverse_two = lax.rsqrt(variance_two + EPSILON)
    norm_one = (centered_one * inverse_one).astype(jnp.bfloat16)
    norm_two = (centered_two * inverse_two).astype(jnp.bfloat16)
    whole_two = lax.all_gather(norm_two, "mp", axis=1, tiled=True)
    total_width = whole_two.shape[1]
    block_index = lax.axis_index("mp")
    slab_index = lax.axis_index("dp")
    shard_cols = total_width // batch_devices
    corr_part = contract_rows(norm_one, whole_two)
    corr_shard = lax.psum_scatter(corr_part, "dp", scatter_dimension=1, tiled=True) / total_rows
    row_ids = block_index * local_width + lax.broadcasted_iota(
        jnp.int32, (local_width, shard_cols), 0
    )
    col_ids = slab_index * shard_cols + lax.broadcasted_iota(
        jnp.int32, (local_width, shard_cols), 1
    )
    grad_shard = jnp.where(
        row_ids == col_ids, -2.0 * (1.0 - corr_shard), 2.0 * OFF_WEIGHT * corr_shard
    ).astype(jnp.bfloat16)
    piece = lax.all_gather(grad_shard, "dp", axis=1, tiled=True)
    upper = times_transposed(whole_two, piece)
    fresh = jnp.dot(norm_one, piece, preferred_element_type=jnp.float32)
    up_two = lax.psum_scatter(
        fresh.astype(jnp.bfloat16), "mp", scatter_dimension=1, tiled=True
    ).astype(jnp.float32)
    normal_one = norm_one.astype(jnp.float32)
    normal_two = norm_two.astype(jnp.float32)
    mean_up_one, cross_one, mean_up_two, cross_two = lax.psum(
        (
            jnp.sum(upper, axis=0),
            jnp.sum(upper * normal_one, axis=0),
            jnp.sum(up_two, axis=0),
            jnp.sum(up_two * normal_two, axis=0),
        ),
        "dp",
    )
    delta_one = (
        inverse_one * (upper - mean_up_one / total_rows - normal_one * (cross_one / total_rows))
    ).astype(jnp.bfloat16)
    delta_two = (
        inverse_two * (up_two - mean_up_two / total_rows - normal_two * (cross_two / total_rows))
    ).astype(jnp.bfloat16)
    partial_one = times_transposed(delta_one, proj_weight)
    partial_two = times_transposed(delta_two, proj_weight)
    summed_one, summed_two = (
        lax.psum_scatter(
            partial_one.astype(jnp.bfloat16), "mp", scatter_dimension=1, tiled=True
        ).astype(jnp.float32),
        lax.psum_scatter(
            partial_two.astype(jnp.bfloat16), "mp", scatter_dimension=1, tiled=True
        ).astype(jnp.float32),
    )
    return (summed_one.astype(jnp.bfloat16), summed_two.astype(jnp.bfloat16))


def solution(mesh):
    placed = (P("dp", "mp"), P("dp", "mp"), P(None, "mp"))

    def whole(view_one, view_two, proj_weight):
        batch, features = view_one.shape
        suits = dict(mesh.shape) == {"dp": DP, "mp": MP}
        suits = suits and batch % (DP * 128) == 0 and 2 * batch <= features and features <= 4096
        return jax.shard_map(
            local_fused if suits else local,
            mesh=mesh, in_specs=placed, out_specs=(P("dp", "mp"), P("dp", "mp")), check_vma=False,
        )(view_one, view_two, proj_weight)

    return whole
```

```python
import jax
import jax.numpy as jnp
from jax import lax
from jax.experimental import pallas as pl
from jax.experimental.pallas import tpu as pltpu
from jax.sharding import PartitionSpec as P

OFF_WEIGHT = 0.0125
EPSILON = 1e-05
MESH = pl.DeviceIdType.MESH
DP, MP = 8, 4
VMEM_KIB = 54700
PARTS = 4


def times_t(left, right):
    return lax.dot_general(
        left, right, (((1,), (1,)), ((), ())), preferred_element_type=jnp.float32
    )


def fused(
    one_hbm, two_hbm, weight_hbm, grad_one_ref, grad_two_ref,
    weight, raw, norm, stat, back, inverse_ref, mean_ref, diagonal, up, own_gram, from_end, from_mid,
    gram, delta, part, from_outer, from_inner,
    view_sem, weight_sem, stat_s, stat_r, back_s, back_r, raw_s, raw_r,
    gram_s, end_r, mid_r, total_s, total_r, part_s, outer_r, inner_r,
):
    rows, width = one_hbm.shape
    total_rows = rows * DP
    half = rows // 2
    bf16, f32 = jnp.bfloat16, jnp.float32
    a, m = lax.axis_index("dp"), lax.axis_index("mp")
    core, along_x, along_y = lax.rem(a, 2), lax.rem(lax.div(a, 2), 2), lax.div(a, 4)

    def peer(r):
        at = a
        if r & 1:
            at = at + 1 - 2 * core
        if r & 2:
            at = at + 2 - 4 * along_x
        if r & 4:
            at = at + 4 - 8 * along_y
        return (at, m)

    low = m < 2
    is_mid = jnp.logical_and(m > 0, m < MP - 1)
    is_end = jnp.logical_not(is_mid)
    inner = (a, jnp.where(low, m + 1, m - 1))
    outer = (a, jnp.where(low, jnp.maximum(m - 1, 0), jnp.minimum(m + 1, MP - 1)))

    def remote(src, dst, send, recv, to):
        return pltpu.make_async_remote_copy(
            src_ref=src, dst_ref=dst, send_sem=send, recv_sem=recv, device_id=to, device_id_type=MESH
        )

    fetch = [
        pltpu.make_async_copy(ref, raw.at[v, pl.ds(0, rows)], view_sem.at[v])
        for v, ref in enumerate((one_hbm, two_hbm))
    ]
    fetch[1].start()
    fetch[0].start()
    load = pltpu.make_async_copy(weight_hbm, weight, weight_sem)
    load.start()

    barrier = pltpu.get_barrier_semaphore()
    for r in range(1, DP):
        pl.semaphore_signal(barrier, inc=1, device_id=peer(r), device_id_type=MESH)
    pl.semaphore_signal(barrier, inc=1, device_id=inner, device_id_type=MESH)

    @pl.when(is_mid)
    def _():
        pl.semaphore_signal(barrier, inc=1, device_id=outer, device_id_type=MESH)

    def raw_copy(v, src, dst, via, h=None):
        size = rows if h is None else half
        skip = 0 if h is None else h * half
        return remote(
            raw.at[v, pl.ds(src * rows + skip, size)], raw.at[v, pl.ds(dst * rows + skip, size)],
            raw_s.at[dst, v, h or 0], raw_r.at[dst, v, h or 0], peer(via),
        )

    def got(v, slot, h=None):
        raw_copy(v, slot, slot, 1, h).wait_recv()

    sent = []

    def give(v, src, dst, via, h=None):
        copy = raw_copy(v, src, dst, via, h)
        copy.start()
        sent.append(copy)

    def give_own(v):
        give(v, 0, 2, 2, 0)
        give(v, 0, 4, 4, 1)
        give(v, 0, 1, 1)
        give(v, 0, 2, 2, 1)
        give(v, 0, 4, 4, 0)

    def give_across(v):
        got(v, 2, 0)
        give(v, 2, 6, 4, 0)
        got(v, 4, 1)
        give(v, 4, 6, 2, 1)

    def block_stat(v):
        x = raw[v, pl.ds(0, rows)].astype(f32)
        mean = jnp.sum(x, axis=0, keepdims=True) / rows
        x = x - mean
        stat[0, pl.ds(2 * v, 1)] = mean
        stat[0, pl.ds(2 * v + 1, 1)] = jnp.sum(x * x, axis=0, keepdims=True)

    def stat_copy(r):
        return remote(stat.at[0], stat.at[r], stat_s.at[r], stat_r.at[r], peer(r))

    for v in (1, 0):
        fetch[v].wait()
        block_stat(v)
    pl.semaphore_wait(barrier, DP + jnp.where(is_mid, 1, 0))
    for r in range(DP - 1, 0, -1):
        stat_copy(r).start()
    give_own(1)
    for r in range(1, DP):
        stat_copy(r).wait_recv()
    for v in range(2):
        means = [stat[r, pl.ds(2 * v, 1)] for r in range(DP)]
        mean = sum(means) / DP
        square = sum(stat[r, pl.ds(2 * v + 1, 1)] for r in range(DP))
        square = square + rows * sum((one - mean) * (one - mean) for one in means)
        mean_ref[pl.ds(v, 1)] = mean
        inverse_ref[pl.ds(v, 1)] = lax.rsqrt(square / total_rows + EPSILON)

    def normalize(v, slot):
        x = raw[v, pl.ds(slot * rows, rows)].astype(f32)
        norm[v, pl.ds(slot * rows, rows)] = (
            (x - mean_ref[pl.ds(v, 1)]) * inverse_ref[pl.ds(v, 1)]
        ).astype(bf16)

    chunks = ((1, 0), (1, 1), (1, 2), (1, 3), (0, 0), (0, 1), (0, 2), (0, 3))
    wide = 2 * rows

    def end_copy(k):
        return remote(own_gram.at[k], from_end.at[k], gram_s.at[k], end_r.at[k], inner)

    def mid_copy(k):
        return remote(own_gram.at[k], from_mid.at[k], gram_s.at[k], mid_r.at[k], inner)

    def total_copy(k):
        return remote(gram.at[k], gram.at[k], total_s.at[k], total_r.at[k], outer)

    def own(k):
        v, p = chunks[k]
        own_gram[k] = times_t(norm[v, pl.ds(0, rows)], norm[v, pl.ds(p * wide, wide)]).astype(bf16)

        @pl.when(is_end)
        def _():
            end_copy(k).start()

    def across(k):
        @pl.when(is_mid)
        def _():
            end_copy(k).wait_recv()
            own_gram[k] = (own_gram[k].astype(f32) + from_end[k].astype(f32)).astype(bf16)
            mid_copy(k).start()

    def back_out(k):
        @pl.when(is_mid)
        def _():
            mid_copy(k).wait_recv()
            gram[k] = (own_gram[k].astype(f32) + from_mid[k].astype(f32)).astype(bf16)
            total_copy(k).start()

    def use(k, slots=(0, 1)):
        v, p = chunks[k]

        if slots[0] == 0:
            @pl.when(is_end)
            def _():
                total_copy(k).wait_recv()

        skip, size = slots[0] * rows, len(slots) * rows
        product = jnp.dot(
            gram[k, :, pl.ds(skip, size)], norm[1 - v, pl.ds(p * wide + skip, size)],
            preferred_element_type=f32,
        )
        if p == 0:
            up[1 - v] = product
        else:
            up[1 - v] += product

    def match(p, slots=(0, 1)):
        at = pl.ds(p * wide + slots[0] * rows, len(slots) * rows)
        both = norm[0, at].astype(f32) * norm[1, at].astype(f32)
        both = jnp.sum(both, axis=0, keepdims=True)
        diagonal[pl.ds(0, 1)] = both if p == 0 else diagonal[pl.ds(0, 1)] + both

    def back_copy(v, r):
        return remote(back.at[v, 0], back.at[v, r], back_s.at[v, r], back_r.at[v, r], peer(r))

    def upstream(v):
        diag = diagonal[pl.ds(0, 1)] / total_rows
        slope = 2.0 * (diag - 1.0) - 2.0 * OFF_WEIGHT * diag
        mine = norm[v, pl.ds(0, rows)].astype(f32)
        other = norm[1 - v, pl.ds(0, rows)].astype(f32)
        value = up[v] * (2.0 * OFF_WEIGHT / total_rows) + other * slope
        up[v] = value
        back[v, 0, pl.ds(0, 1)] = jnp.sum(value, axis=0, keepdims=True)
        back[v, 0, pl.ds(1, 1)] = jnp.sum(value * mine, axis=0, keepdims=True)
        for r in range(DP - 1, 0, -1):
            back_copy(v, r).start()

    def through_norm(v):
        for r in range(1, DP):
            back_copy(v, r).wait_recv()
        mean_up = sum(back[v, r, pl.ds(0, 1)] for r in range(DP)) / total_rows
        cross = sum(back[v, r, pl.ds(1, 1)] for r in range(DP)) / total_rows
        mine = norm[v, pl.ds(0, rows)].astype(f32)
        delta[v] = (inverse_ref[pl.ds(v, 1)] * (up[v] - mean_up - mine * cross)).astype(bf16)

    slim = width // PARTS

    def outward(v, j, c):
        return remote(
            part.at[v, j, c], from_outer.at[v, j, c], part_s.at[v, j, c], outer_r.at[v, j, c], inner
        )

    def over(v, j, c):
        return remote(
            part.at[v, j, c], from_inner.at[v, 3 - j, c], part_s.at[v, j, c], inner_r.at[v, 3 - j, c], inner
        )

    def homeward(v, c):
        return remote(
            part.at[v, 0, c], from_inner.at[v, 0, c], part_s.at[v, 0, c], inner_r.at[v, 0, c], outer
        )

    def product(v, j, c):
        block = jnp.where(low, j, MP - 1 - j)
        start = pl.multiple_of(block * width + c * slim, slim)
        return times_t(delta[v], weight[pl.ds(start, slim)])

    def send_out(v):
        @pl.when(is_end)
        def _():
            @pl.loop(0, (MP - 1) * PARTS)
            def _(step):
                j = MP - 1 - lax.div(step, PARTS)
                c = lax.rem(step, PARTS)
                part[v, j, c] = product(v, j, c).astype(bf16)
                outward(v, j, c).start()

    def pass_on(v, j, c):
        mine = product(v, j, c)
        outward(v, j, c).wait_recv()
        part[v, j, c] = (mine + from_outer[v, j, c].astype(f32)).astype(bf16)
        over(v, j, c).start()

    def pass_home(v, c):
        mine = product(v, 0, c)
        over(v, 3, c).wait_recv()
        part[v, 0, c] = (mine + from_inner[v, 0, c].astype(f32)).astype(bf16)
        homeward(v, c).start()

    normalize(1, 0)
    got(1, 1)
    normalize(1, 1)
    own(0)
    give_across(1)
    give_own(0)
    got(1, 2, 1)
    give(1, 2, 3, 1)
    got(1, 4, 0)
    give(1, 4, 5, 1)
    normalize(1, 2)
    normalize(1, 4)
    across(0)
    got(1, 3)
    normalize(1, 3)
    own(1)
    got(1, 5)
    normalize(1, 5)
    own(2)
    back_out(0)
    normalize(0, 0)
    got(0, 1)
    normalize(0, 1)
    got(1, 6, 0)
    got(1, 6, 1)
    give(1, 6, 7, 1)
    normalize(1, 6)
    across(1)
    across(2)
    got(1, 7)
    normalize(1, 7)
    own(3)
    own(4)
    match(0)

    give_across(0)
    back_out(1)
    back_out(2)
    use(0)
    across(3)
    across(4)
    got(0, 2, 1)
    give(0, 2, 3, 1)
    got(0, 4, 0)
    give(0, 4, 5, 1)
    normalize(0, 2)
    normalize(0, 4)
    got(0, 3)
    normalize(0, 3)
    own(5)
    back_out(3)
    use(1)
    got(0, 5)
    normalize(0, 5)
    own(6)
    back_out(4)
    use(2)
    match(1)
    match(2)
    across(5)
    across(6)
    got(0, 6, 0)
    give(0, 6, 7, 1, 0)
    got(0, 6, 1)
    give(0, 6, 7, 1, 1)
    normalize(0, 6)
    match(3, (0,))
    use(3, (0,))
    got(0, 7, 0)
    got(0, 7, 1)
    normalize(0, 7)
    match(3, (1,))
    use(3, (1,))
    upstream(0)
    own(7)
    back_out(5)
    back_out(6)
    use(4)
    load.wait()
    through_norm(0)
    across(7)
    send_out(0)

    back_out(7)
    use(5)
    use(6)
    use(7)
    upstream(1)

    @pl.when(is_mid)
    def _():
        @pl.loop(0, PARTS)
        def _(c):
            pass_on(0, MP - 1, c)

    through_norm(1)
    send_out(1)

    outs = (grad_one_ref, grad_two_ref)

    def all_left():
        for r in range(1, DP):
            stat_copy(r).wait_send()
            for v in range(2):
                back_copy(v, r).wait_send()
        for copy in sent:
            copy.wait_send()
        for k in range(len(chunks)):
            end_copy(k).wait_send()

    def parts_left(v, blocks):
        for j in blocks:
            for c in range(PARTS):
                outward(v, j, c).wait_send()

    @pl.when(is_end)
    def _():
        all_left()
        for v in range(2):
            @pl.loop(0, PARTS)
            def _(c):
                mine = product(v, 0, c)
                homeward(v, c).wait_recv()
                outs[v][:, pl.ds(pl.multiple_of(c * slim, slim), slim)] = (
                    mine + from_inner[v, 0, c].astype(f32)
                ).astype(bf16)

            parts_left(v, (3, 2, 1))

    @pl.when(is_mid)
    def _():
        for v in range(2):
            if v == 1:
                @pl.loop(0, PARTS)
                def _(c):
                    pass_on(v, MP - 1, c)

            @pl.loop(0, PARTS)
            def _(c):
                pass_home(v, c)
                pass_on(v, MP - 2, c)

            if v == 0:
                all_left()
                for k in range(len(chunks)):
                    total_copy(k).wait_send()
            parts_left(v, (3, 0))

            @pl.loop(0, PARTS)
            def _(c):
                mine = product(v, 1, c)
                over(v, 2, c).wait_recv()
                mine = mine + from_inner[v, 1, c].astype(f32)
                outward(v, 1, c).wait_recv()
                outs[v][:, pl.ds(pl.multiple_of(c * slim, slim), slim)] = (
                    mine + from_outer[v, 1, c].astype(f32)
                ).astype(bf16)

            parts_left(v, (2,))


def local_fused(view_one, view_two, proj_weight):
    rows, width = view_one.shape
    bf16, f32 = jnp.bfloat16, jnp.float32
    dma = pltpu.SemaphoreType.DMA
    slim = width // PARTS
    out = jax.ShapeDtypeStruct((rows, width), bf16)
    vmem = pl.BlockSpec(memory_space=pltpu.VMEM)
    return pl.pallas_call(
        fused,
        out_shape=(out, out),
        in_specs=[pl.BlockSpec(memory_space=pltpu.HBM)] * 3,
        out_specs=(vmem, vmem),
        scratch_shapes=[
            pltpu.VMEM(proj_weight.shape, bf16),
            pltpu.VMEM((2, DP * rows, width), bf16),
            pltpu.VMEM((2, DP * rows, width), bf16),
            pltpu.VMEM((DP, 4, width), f32),
            pltpu.VMEM((2, DP, 2, width), f32),
            pltpu.VMEM((8, width), f32),
            pltpu.VMEM((8, width), f32),
            pltpu.VMEM((8, width), f32),
            pltpu.VMEM((2, rows, width), f32),
            pltpu.VMEM((8, rows, 2 * rows), bf16),
            pltpu.VMEM((8, rows, 2 * rows), bf16),
            pltpu.VMEM((8, rows, 2 * rows), bf16),
            pltpu.VMEM((8, rows, 2 * rows), bf16),
            pltpu.VMEM((2, rows, width), bf16),
            pltpu.VMEM((2, MP, PARTS, rows, slim), bf16),
            pltpu.VMEM((2, MP, PARTS, rows, slim), bf16),
            pltpu.VMEM((2, 2, PARTS, rows, slim), bf16),
            dma((2,)),
            dma(()),
            dma((DP,)), dma((DP,)), dma((2, DP)), dma((2, DP)),
            dma((DP, 2, 2)), dma((DP, 2, 2)),
            dma((8,)), dma((8,)), dma((8,)), dma((8,)), dma((8,)),
            dma((2, MP, PARTS)), dma((2, MP, PARTS)), dma((2, 2, PARTS)),
        ],
        compiler_params=pltpu.CompilerParams(
            collective_id=0, has_side_effects=True, vmem_limit_bytes=VMEM_KIB * 1024
        ),
        cost_estimate=pl.CostEstimate(
            flops=4 * rows * width * (2 * DP * rows + MP * width),
            bytes_accessed=2 * (MP * width * width + 4 * rows * width),
            transcendentals=0,
        ),
    )(view_one, view_two, proj_weight)


def contract_rows(left, right):
    return lax.dot_general(
        left, right, (((0,), (0,)), ((), ())), preferred_element_type=jnp.float32
    )


def times_transposed(left, right):
    return lax.dot_general(
        left, right, (((1,), (1,)), ((), ())), preferred_element_type=jnp.float32
    )


def local(view_one, view_two, proj_weight):
    row_count, local_width = view_one.shape
    batch_devices = lax.axis_size("dp")
    total_rows = row_count * batch_devices
    first = view_one.astype(jnp.float32)
    second = view_two.astype(jnp.float32)
    sum_one, sum_two = lax.psum((jnp.sum(first, axis=0), jnp.sum(second, axis=0)), "dp")
    center_one = sum_one / total_rows
    center_two = sum_two / total_rows
    centered_one = first - center_one
    centered_two = second - center_two
    square_one, square_two = lax.psum(
        (
            jnp.sum(centered_one * centered_one, axis=0),
            jnp.sum(centered_two * centered_two, axis=0),
        ),
        "dp",
    )
    variance_one = square_one / total_rows
    variance_two = square_two / total_rows
    inverse_one = lax.rsqrt(variance_one + EPSILON)
    inverse_two = lax.rsqrt(variance_two + EPSILON)
    norm_one = (centered_one * inverse_one).astype(jnp.bfloat16)
    norm_two = (centered_two * inverse_two).astype(jnp.bfloat16)
    whole_two = lax.all_gather(norm_two, "mp", axis=1, tiled=True)
    total_width = whole_two.shape[1]
    block_index = lax.axis_index("mp")
    slab_index = lax.axis_index("dp")
    shard_cols = total_width // batch_devices
    corr_part = contract_rows(norm_one, whole_two)
    corr_shard = lax.psum_scatter(corr_part, "dp", scatter_dimension=1, tiled=True) / total_rows
    row_ids = block_index * local_width + lax.broadcasted_iota(
        jnp.int32, (local_width, shard_cols), 0
    )
    col_ids = slab_index * shard_cols + lax.broadcasted_iota(
        jnp.int32, (local_width, shard_cols), 1
    )
    grad_shard = jnp.where(
        row_ids == col_ids, -2.0 * (1.0 - corr_shard), 2.0 * OFF_WEIGHT * corr_shard
    ).astype(jnp.bfloat16)
    piece = lax.all_gather(grad_shard, "dp", axis=1, tiled=True)
    upper = times_transposed(whole_two, piece)
    fresh = jnp.dot(norm_one, piece, preferred_element_type=jnp.float32)
    up_two = lax.psum_scatter(
        fresh.astype(jnp.bfloat16), "mp", scatter_dimension=1, tiled=True
    ).astype(jnp.float32)
    normal_one = norm_one.astype(jnp.float32)
    normal_two = norm_two.astype(jnp.float32)
    mean_up_one, cross_one, mean_up_two, cross_two = lax.psum(
        (
            jnp.sum(upper, axis=0),
            jnp.sum(upper * normal_one, axis=0),
            jnp.sum(up_two, axis=0),
            jnp.sum(up_two * normal_two, axis=0),
        ),
        "dp",
    )
    delta_one = (
        inverse_one * (upper - mean_up_one / total_rows - normal_one * (cross_one / total_rows))
    ).astype(jnp.bfloat16)
    delta_two = (
        inverse_two * (up_two - mean_up_two / total_rows - normal_two * (cross_two / total_rows))
    ).astype(jnp.bfloat16)
    partial_one = times_transposed(delta_one, proj_weight)
    partial_two = times_transposed(delta_two, proj_weight)
    summed_one, summed_two = (
        lax.psum_scatter(
            partial_one.astype(jnp.bfloat16), "mp", scatter_dimension=1, tiled=True
        ).astype(jnp.float32),
        lax.psum_scatter(
            partial_two.astype(jnp.bfloat16), "mp", scatter_dimension=1, tiled=True
        ).astype(jnp.float32),
    )
    return (summed_one.astype(jnp.bfloat16), summed_two.astype(jnp.bfloat16))


def solution(mesh):
    placed = (P("dp", "mp"), P("dp", "mp"), P(None, "mp"))

    def whole(view_one, view_two, proj_weight):
        batch, features = view_one.shape
        suits = dict(mesh.shape) == {"dp": DP, "mp": MP}
        suits = suits and batch % (DP * 128) == 0 and 2 * batch <= features and features <= 4096
        return jax.shard_map(
            local_fused if suits else local,
            mesh=mesh, in_specs=placed, out_specs=(P("dp", "mp"), P("dp", "mp")), check_vma=False,
        )(view_one, view_two, proj_weight)

    return whole
```

```python
import jax
import jax.numpy as jnp
from jax import lax
from jax.experimental import pallas as pl
from jax.experimental.pallas import tpu as pltpu
from jax.sharding import PartitionSpec as P

OFF_WEIGHT = 0.0125
EPSILON = 1e-05
MESH = pl.DeviceIdType.MESH
DP, MP = 8, 4
VMEM_KIB = 54700
PARTS = 2


def times_t(left, right):
    return lax.dot_general(
        left, right, (((1,), (1,)), ((), ())), preferred_element_type=jnp.float32
    )


def fused(
    one_hbm, two_hbm, weight_hbm, grad_one_ref, grad_two_ref,
    weight, raw, norm, stat, back, inverse_ref, mean_ref, diagonal, up, own_gram, from_end, from_mid,
    gram, delta, part, from_outer, from_inner,
    view_sem, weight_sem, stat_s, stat_r, back_s, back_r, raw_s, raw_r,
    gram_s, end_r, mid_r, total_s, total_r, part_s, outer_r, inner_r,
):
    rows, width = one_hbm.shape
    total_rows = rows * DP
    half = rows // 2
    bf16, f32 = jnp.bfloat16, jnp.float32
    a, m = lax.axis_index("dp"), lax.axis_index("mp")
    core, along_x, along_y = lax.rem(a, 2), lax.rem(lax.div(a, 2), 2), lax.div(a, 4)

    def peer(r):
        at = a
        if r & 1:
            at = at + 1 - 2 * core
        if r & 2:
            at = at + 2 - 4 * along_x
        if r & 4:
            at = at + 4 - 8 * along_y
        return (at, m)

    low = m < 2
    is_mid = jnp.logical_and(m > 0, m < MP - 1)
    is_end = jnp.logical_not(is_mid)
    inner = (a, jnp.where(low, m + 1, m - 1))
    outer = (a, jnp.where(low, jnp.maximum(m - 1, 0), jnp.minimum(m + 1, MP - 1)))

    def remote(src, dst, send, recv, to):
        return pltpu.make_async_remote_copy(
            src_ref=src, dst_ref=dst, send_sem=send, recv_sem=recv, device_id=to, device_id_type=MESH
        )

    fetch = [
        pltpu.make_async_copy(ref, raw.at[v, pl.ds(0, rows)], view_sem.at[v])
        for v, ref in enumerate((one_hbm, two_hbm))
    ]
    fetch[1].start()
    fetch[0].start()
    load = pltpu.make_async_copy(weight_hbm, weight, weight_sem)

    barrier = pltpu.get_barrier_semaphore()
    for r in range(1, DP):
        pl.semaphore_signal(barrier, inc=1, device_id=peer(r), device_id_type=MESH)
    pl.semaphore_signal(barrier, inc=1, device_id=inner, device_id_type=MESH)

    @pl.when(is_mid)
    def _():
        pl.semaphore_signal(barrier, inc=1, device_id=outer, device_id_type=MESH)

    def raw_copy(v, src, dst, via, h=None):
        size = rows if h is None else half
        skip = 0 if h is None else h * half
        return remote(
            raw.at[v, pl.ds(src * rows + skip, size)], raw.at[v, pl.ds(dst * rows + skip, size)],
            raw_s.at[dst, v, h or 0], raw_r.at[dst, v, h or 0], peer(via),
        )

    def got(v, slot, h=None):
        raw_copy(v, slot, slot, 1, h).wait_recv()

    sent = []

    def give(v, src, dst, via, h=None):
        copy = raw_copy(v, src, dst, via, h)
        copy.start()
        sent.append(copy)

    def give_own(v):
        give(v, 0, 2, 2, 0)
        give(v, 0, 4, 4, 1)
        give(v, 0, 1, 1)
        give(v, 0, 2, 2, 1)
        give(v, 0, 4, 4, 0)

    def give_across(v):
        got(v, 2, 0)
        give(v, 2, 6, 4, 0)
        got(v, 4, 1)
        give(v, 4, 6, 2, 1)

    def block_stat(v):
        x = raw[v, pl.ds(0, rows)].astype(f32)
        mean = jnp.sum(x, axis=0, keepdims=True) / rows
        x = x - mean
        stat[0, pl.ds(2 * v, 1)] = mean
        stat[0, pl.ds(2 * v + 1, 1)] = jnp.sum(x * x, axis=0, keepdims=True)

    def stat_copy(r):
        return remote(stat.at[0], stat.at[r], stat_s.at[r], stat_r.at[r], peer(r))

    for v in (1, 0):
        fetch[v].wait()
        block_stat(v)
    pl.semaphore_wait(barrier, DP + jnp.where(is_mid, 1, 0))
    for r in range(DP - 1, 0, -1):
        stat_copy(r).start()
    give_own(1)
    load.start()
    for r in range(1, DP):
        stat_copy(r).wait_recv()
    for v in range(2):
        means = [stat[r, pl.ds(2 * v, 1)] for r in range(DP)]
        mean = sum(means) / DP
        square = sum(stat[r, pl.ds(2 * v + 1, 1)] for r in range(DP))
        square = square + rows * sum((one - mean) * (one - mean) for one in means)
        mean_ref[pl.ds(v, 1)] = mean
        inverse_ref[pl.ds(v, 1)] = lax.rsqrt(square / total_rows + EPSILON)

    def normalize(v, slot):
        x = raw[v, pl.ds(slot * rows, rows)].astype(f32)
        norm[v, pl.ds(slot * rows, rows)] = (
            (x - mean_ref[pl.ds(v, 1)]) * inverse_ref[pl.ds(v, 1)]
        ).astype(bf16)

    chunks = ((1, 0), (1, 1), (1, 2), (1, 3), (0, 0), (0, 1), (0, 2), (0, 3))
    wide = 2 * rows

    def end_copy(k):
        return remote(own_gram.at[k], from_end.at[k], gram_s.at[k], end_r.at[k], inner)

    def mid_copy(k):
        return remote(own_gram.at[k], from_mid.at[k], gram_s.at[k], mid_r.at[k], inner)

    def total_copy(k):
        return remote(gram.at[k], gram.at[k], total_s.at[k], total_r.at[k], outer)

    def own(k):
        v, p = chunks[k]
        own_gram[k] = times_t(norm[v, pl.ds(0, rows)], norm[v, pl.ds(p * wide, wide)]).astype(bf16)

        @pl.when(is_end)
        def _():
            end_copy(k).start()

    def across(k):
        @pl.when(is_mid)
        def _():
            end_copy(k).wait_recv()
            own_gram[k] = (own_gram[k].astype(f32) + from_end[k].astype(f32)).astype(bf16)
            mid_copy(k).start()

    def back_out(k):
        @pl.when(is_mid)
        def _():
            mid_copy(k).wait_recv()
            gram[k] = (own_gram[k].astype(f32) + from_mid[k].astype(f32)).astype(bf16)
            total_copy(k).start()

    def use(k, slots=(0, 1)):
        v, p = chunks[k]

        if slots[0] == 0:
            @pl.when(is_end)
            def _():
                total_copy(k).wait_recv()

        skip, size = slots[0] * rows, len(slots) * rows
        product = jnp.dot(
            gram[k, :, pl.ds(skip, size)], norm[1 - v, pl.ds(p * wide + skip, size)],
            preferred_element_type=f32,
        )
        if p == 0:
            up[1 - v] = product
        else:
            up[1 - v] += product

    def match(p, slots=(0, 1)):
        at = pl.ds(p * wide + slots[0] * rows, len(slots) * rows)
        both = norm[0, at].astype(f32) * norm[1, at].astype(f32)
        both = jnp.sum(both, axis=0, keepdims=True)
        diagonal[pl.ds(0, 1)] = both if p == 0 else diagonal[pl.ds(0, 1)] + both

    def back_copy(v, r):
        return remote(back.at[v, 0], back.at[v, r], back_s.at[v, r], back_r.at[v, r], peer(r))

    def upstream(v):
        diag = diagonal[pl.ds(0, 1)] / total_rows
        slope = 2.0 * (diag - 1.0) - 2.0 * OFF_WEIGHT * diag
        mine = norm[v, pl.ds(0, rows)].astype(f32)
        other = norm[1 - v, pl.ds(0, rows)].astype(f32)
        value = up[v] * (2.0 * OFF_WEIGHT / total_rows) + other * slope
        up[v] = value
        back[v, 0, pl.ds(0, 1)] = jnp.sum(value, axis=0, keepdims=True)
        back[v, 0, pl.ds(1, 1)] = jnp.sum(value * mine, axis=0, keepdims=True)
        for r in range(DP - 1, 0, -1):
            back_copy(v, r).start()

    def through_norm(v):
        for r in range(1, DP):
            back_copy(v, r).wait_recv()
        mean_up = sum(back[v, r, pl.ds(0, 1)] for r in range(DP)) / total_rows
        cross = sum(back[v, r, pl.ds(1, 1)] for r in range(DP)) / total_rows
        mine = norm[v, pl.ds(0, rows)].astype(f32)
        delta[v] = (inverse_ref[pl.ds(v, 1)] * (up[v] - mean_up - mine * cross)).astype(bf16)

    slim = width // PARTS

    def outward(v, j, c):
        return remote(
            part.at[v, j, c], from_outer.at[v, j, c], part_s.at[v, j, c], outer_r.at[v, j, c], inner
        )

    def over(v, j, c):
        return remote(
            part.at[v, j, c], from_inner.at[v, 3 - j, c], part_s.at[v, j, c], inner_r.at[v, 3 - j, c], inner
        )

    def homeward(v, c):
        return remote(
            part.at[v, 0, c], from_inner.at[v, 0, c], part_s.at[v, 0, c], inner_r.at[v, 0, c], outer
        )

    def product(v, j, c):
        block = jnp.where(low, j, MP - 1 - j)
        start = pl.multiple_of(block * width + c * slim, slim)
        return times_t(delta[v], weight[pl.ds(start, slim)])

    def send_out(v):
        @pl.when(is_end)
        def _():
            @pl.loop(0, (MP - 1) * PARTS)
            def _(step):
                j = MP - 1 - lax.div(step, PARTS)
                c = lax.rem(step, PARTS)
                part[v, j, c] = product(v, j, c).astype(bf16)
                outward(v, j, c).start()

    def pass_on(v, j, c):
        mine = product(v, j, c)
        outward(v, j, c).wait_recv()
        part[v, j, c] = (mine + from_outer[v, j, c].astype(f32)).astype(bf16)
        over(v, j, c).start()

    def pass_home(v, c):
        mine = product(v, 0, c)
        over(v, 3, c).wait_recv()
        part[v, 0, c] = (mine + from_inner[v, 0, c].astype(f32)).astype(bf16)
        homeward(v, c).start()

    normalize(1, 0)
    got(1, 1)
    normalize(1, 1)
    own(0)
    give_across(1)
    give_own(0)
    got(1, 2, 1)
    give(1, 2, 3, 1)
    got(1, 4, 0)
    give(1, 4, 5, 1)
    normalize(1, 2)
    normalize(1, 4)
    across(0)
    got(1, 3)
    normalize(1, 3)
    own(1)
    got(1, 5)
    normalize(1, 5)
    own(2)
    back_out(0)
    normalize(0, 0)
    got(0, 1)
    normalize(0, 1)
    got(1, 6, 0)
    got(1, 6, 1)
    give(1, 6, 7, 1)
    normalize(1, 6)
    across(1)
    across(2)
    got(1, 7)
    normalize(1, 7)
    own(3)
    own(4)
    match(0)

    give_across(0)
    back_out(1)
    back_out(2)
    use(0)
    across(3)
    across(4)
    got(0, 2, 1)
    give(0, 2, 3, 1)
    got(0, 4, 0)
    give(0, 4, 5, 1)
    normalize(0, 2)
    normalize(0, 4)
    got(0, 3)
    normalize(0, 3)
    own(5)
    back_out(3)
    use(1)
    got(0, 5)
    normalize(0, 5)
    own(6)
    back_out(4)
    use(2)
    match(1)
    match(2)
    across(5)
    across(6)
    got(0, 6, 0)
    give(0, 6, 7, 1, 0)
    got(0, 6, 1)
    give(0, 6, 7, 1, 1)
    normalize(0, 6)
    match(3, (0,))
    use(3, (0,))
    got(0, 7, 0)
    got(0, 7, 1)
    normalize(0, 7)
    match(3, (1,))
    use(3, (1,))
    upstream(0)
    own(7)
    back_out(5)
    back_out(6)
    use(4)
    load.wait()
    through_norm(0)
    across(7)
    send_out(0)

    back_out(7)
    use(5)
    use(6)
    use(7)
    upstream(1)

    @pl.when(is_mid)
    def _():
        @pl.loop(0, PARTS)
        def _(c):
            pass_on(0, MP - 1, c)

    through_norm(1)
    send_out(1)

    outs = (grad_one_ref, grad_two_ref)

    def all_left():
        for r in range(1, DP):
            stat_copy(r).wait_send()
            for v in range(2):
                back_copy(v, r).wait_send()
        for copy in sent:
            copy.wait_send()
        for k in range(len(chunks)):
            end_copy(k).wait_send()

    def parts_left(v, blocks):
        for j in blocks:
            for c in range(PARTS):
                outward(v, j, c).wait_send()

    @pl.when(is_end)
    def _():
        all_left()
        for v in range(2):
            @pl.loop(0, PARTS)
            def _(c):
                mine = product(v, 0, c)
                homeward(v, c).wait_recv()
                outs[v][:, pl.ds(pl.multiple_of(c * slim, slim), slim)] = (
                    mine + from_inner[v, 0, c].astype(f32)
                ).astype(bf16)

            parts_left(v, (3, 2, 1))

    @pl.when(is_mid)
    def _():
        for v in range(2):
            if v == 1:
                @pl.loop(0, PARTS)
                def _(c):
                    pass_on(v, MP - 1, c)

            @pl.loop(0, PARTS)
            def _(c):
                pass_home(v, c)
                pass_on(v, MP - 2, c)

            if v == 0:
                all_left()
                for k in range(len(chunks)):
                    total_copy(k).wait_send()
            parts_left(v, (3, 0))

            @pl.loop(0, PARTS)
            def _(c):
                mine = product(v, 1, c)
                over(v, 2, c).wait_recv()
                mine = mine + from_inner[v, 1, c].astype(f32)
                outward(v, 1, c).wait_recv()
                outs[v][:, pl.ds(pl.multiple_of(c * slim, slim), slim)] = (
                    mine + from_outer[v, 1, c].astype(f32)
                ).astype(bf16)

            parts_left(v, (2,))


def local_fused(view_one, view_two, proj_weight):
    rows, width = view_one.shape
    bf16, f32 = jnp.bfloat16, jnp.float32
    dma = pltpu.SemaphoreType.DMA
    slim = width // PARTS
    out = jax.ShapeDtypeStruct((rows, width), bf16)
    vmem = pl.BlockSpec(memory_space=pltpu.VMEM)
    return pl.pallas_call(
        fused,
        out_shape=(out, out),
        in_specs=[pl.BlockSpec(memory_space=pltpu.HBM)] * 3,
        out_specs=(vmem, vmem),
        scratch_shapes=[
            pltpu.VMEM(proj_weight.shape, bf16),
            pltpu.VMEM((2, DP * rows, width), bf16),
            pltpu.VMEM((2, DP * rows, width), bf16),
            pltpu.VMEM((DP, 4, width), f32),
            pltpu.VMEM((2, DP, 2, width), f32),
            pltpu.VMEM((8, width), f32),
            pltpu.VMEM((8, width), f32),
            pltpu.VMEM((8, width), f32),
            pltpu.VMEM((2, rows, width), f32),
            pltpu.VMEM((8, rows, 2 * rows), bf16),
            pltpu.VMEM((8, rows, 2 * rows), bf16),
            pltpu.VMEM((8, rows, 2 * rows), bf16),
            pltpu.VMEM((8, rows, 2 * rows), bf16),
            pltpu.VMEM((2, rows, width), bf16),
            pltpu.VMEM((2, MP, PARTS, rows, slim), bf16),
            pltpu.VMEM((2, MP, PARTS, rows, slim), bf16),
            pltpu.VMEM((2, 2, PARTS, rows, slim), bf16),
            dma((2,)),
            dma(()),
            dma((DP,)), dma((DP,)), dma((2, DP)), dma((2, DP)),
            dma((DP, 2, 2)), dma((DP, 2, 2)),
            dma((8,)), dma((8,)), dma((8,)), dma((8,)), dma((8,)),
            dma((2, MP, PARTS)), dma((2, MP, PARTS)), dma((2, 2, PARTS)),
        ],
        compiler_params=pltpu.CompilerParams(
            collective_id=0, has_side_effects=True, vmem_limit_bytes=VMEM_KIB * 1024
        ),
        cost_estimate=pl.CostEstimate(
            flops=4 * rows * width * (2 * DP * rows + MP * width),
            bytes_accessed=2 * (MP * width * width + 4 * rows * width),
            transcendentals=0,
        ),
    )(view_one, view_two, proj_weight)


def contract_rows(left, right):
    return lax.dot_general(
        left, right, (((0,), (0,)), ((), ())), preferred_element_type=jnp.float32
    )


def times_transposed(left, right):
    return lax.dot_general(
        left, right, (((1,), (1,)), ((), ())), preferred_element_type=jnp.float32
    )


def local(view_one, view_two, proj_weight):
    row_count, local_width = view_one.shape
    batch_devices = lax.axis_size("dp")
    total_rows = row_count * batch_devices
    first = view_one.astype(jnp.float32)
    second = view_two.astype(jnp.float32)
    sum_one, sum_two = lax.psum((jnp.sum(first, axis=0), jnp.sum(second, axis=0)), "dp")
    center_one = sum_one / total_rows
    center_two = sum_two / total_rows
    centered_one = first - center_one
    centered_two = second - center_two
    square_one, square_two = lax.psum(
        (
            jnp.sum(centered_one * centered_one, axis=0),
            jnp.sum(centered_two * centered_two, axis=0),
        ),
        "dp",
    )
    variance_one = square_one / total_rows
    variance_two = square_two / total_rows
    inverse_one = lax.rsqrt(variance_one + EPSILON)
    inverse_two = lax.rsqrt(variance_two + EPSILON)
    norm_one = (centered_one * inverse_one).astype(jnp.bfloat16)
    norm_two = (centered_two * inverse_two).astype(jnp.bfloat16)
    whole_two = lax.all_gather(norm_two, "mp", axis=1, tiled=True)
    total_width = whole_two.shape[1]
    block_index = lax.axis_index("mp")
    slab_index = lax.axis_index("dp")
    shard_cols = total_width // batch_devices
    corr_part = contract_rows(norm_one, whole_two)
    corr_shard = lax.psum_scatter(corr_part, "dp", scatter_dimension=1, tiled=True) / total_rows
    row_ids = block_index * local_width + lax.broadcasted_iota(
        jnp.int32, (local_width, shard_cols), 0
    )
    col_ids = slab_index * shard_cols + lax.broadcasted_iota(
        jnp.int32, (local_width, shard_cols), 1
    )
    grad_shard = jnp.where(
        row_ids == col_ids, -2.0 * (1.0 - corr_shard), 2.0 * OFF_WEIGHT * corr_shard
    ).astype(jnp.bfloat16)
    piece = lax.all_gather(grad_shard, "dp", axis=1, tiled=True)
    upper = times_transposed(whole_two, piece)
    fresh = jnp.dot(norm_one, piece, preferred_element_type=jnp.float32)
    up_two = lax.psum_scatter(
        fresh.astype(jnp.bfloat16), "mp", scatter_dimension=1, tiled=True
    ).astype(jnp.float32)
    normal_one = norm_one.astype(jnp.float32)
    normal_two = norm_two.astype(jnp.float32)
    mean_up_one, cross_one, mean_up_two, cross_two = lax.psum(
        (
            jnp.sum(upper, axis=0),
            jnp.sum(upper * normal_one, axis=0),
            jnp.sum(up_two, axis=0),
            jnp.sum(up_two * normal_two, axis=0),
        ),
        "dp",
    )
    delta_one = (
        inverse_one * (upper - mean_up_one / total_rows - normal_one * (cross_one / total_rows))
    ).astype(jnp.bfloat16)
    delta_two = (
        inverse_two * (up_two - mean_up_two / total_rows - normal_two * (cross_two / total_rows))
    ).astype(jnp.bfloat16)
    partial_one = times_transposed(delta_one, proj_weight)
    partial_two = times_transposed(delta_two, proj_weight)
    summed_one, summed_two = (
        lax.psum_scatter(
            partial_one.astype(jnp.bfloat16), "mp", scatter_dimension=1, tiled=True
        ).astype(jnp.float32),
        lax.psum_scatter(
            partial_two.astype(jnp.bfloat16), "mp", scatter_dimension=1, tiled=True
        ).astype(jnp.float32),
    )
    return (summed_one.astype(jnp.bfloat16), summed_two.astype(jnp.bfloat16))


def solution(mesh):
    placed = (P("dp", "mp"), P("dp", "mp"), P(None, "mp"))

    def whole(view_one, view_two, proj_weight):
        batch, features = view_one.shape
        suits = dict(mesh.shape) == {"dp": DP, "mp": MP}
        suits = suits and batch % (DP * 128) == 0 and 2 * batch <= features and features <= 4096
        return jax.shard_map(
            local_fused if suits else local,
            mesh=mesh, in_specs=placed, out_specs=(P("dp", "mp"), P("dp", "mp")), check_vma=False,
        )(view_one, view_two, proj_weight)

    return whole
```

```python
import jax
import jax.numpy as jnp
from jax import lax
from jax.experimental import pallas as pl
from jax.experimental.pallas import tpu as pltpu
from jax.sharding import PartitionSpec as P

OFF_WEIGHT = 0.0125
EPSILON = 1e-05
MESH = pl.DeviceIdType.MESH
DP, MP = 8, 4
VMEM_KIB = 54700
PARTS = 8


def times_t(left, right):
    return lax.dot_general(
        left, right, (((1,), (1,)), ((), ())), preferred_element_type=jnp.float32
    )


def fused(
    one_hbm, two_hbm, weight_hbm, grad_one_ref, grad_two_ref,
    weight, raw, norm, stat, back, inverse_ref, mean_ref, diagonal, up, own_gram, from_end, from_mid,
    gram, delta, part, from_outer, from_inner,
    view_sem, weight_sem, stat_s, stat_r, back_s, back_r, raw_s, raw_r,
    gram_s, end_r, mid_r, total_s, total_r, part_s, outer_r, inner_r,
):
    rows, width = one_hbm.shape
    total_rows = rows * DP
    half = rows // 2
    bf16, f32 = jnp.bfloat16, jnp.float32
    a, m = lax.axis_index("dp"), lax.axis_index("mp")
    core, along_x, along_y = lax.rem(a, 2), lax.rem(lax.div(a, 2), 2), lax.div(a, 4)

    def peer(r):
        at = a
        if r & 1:
            at = at + 1 - 2 * core
        if r & 2:
            at = at + 2 - 4 * along_x
        if r & 4:
            at = at + 4 - 8 * along_y
        return (at, m)

    low = m < 2
    is_mid = jnp.logical_and(m > 0, m < MP - 1)
    is_end = jnp.logical_not(is_mid)
    inner = (a, jnp.where(low, m + 1, m - 1))
    outer = (a, jnp.where(low, jnp.maximum(m - 1, 0), jnp.minimum(m + 1, MP - 1)))

    def remote(src, dst, send, recv, to):
        return pltpu.make_async_remote_copy(
            src_ref=src, dst_ref=dst, send_sem=send, recv_sem=recv, device_id=to, device_id_type=MESH
        )

    fetch = [
        pltpu.make_async_copy(ref, raw.at[v, pl.ds(0, rows)], view_sem.at[v])
        for v, ref in enumerate((one_hbm, two_hbm))
    ]
    fetch[1].start()
    fetch[0].start()
    load = pltpu.make_async_copy(weight_hbm, weight, weight_sem)
    load.start()

    barrier = pltpu.get_barrier_semaphore()
    for r in range(1, DP):
        pl.semaphore_signal(barrier, inc=1, device_id=peer(r), device_id_type=MESH)
    pl.semaphore_signal(barrier, inc=1, device_id=inner, device_id_type=MESH)

    @pl.when(is_mid)
    def _():
        pl.semaphore_signal(barrier, inc=1, device_id=outer, device_id_type=MESH)

    def raw_copy(v, src, dst, via, h=None):
        size = rows if h is None else half
        skip = 0 if h is None else h * half
        return remote(
            raw.at[v, pl.ds(src * rows + skip, size)], raw.at[v, pl.ds(dst * rows + skip, size)],
            raw_s.at[dst, v, h or 0], raw_r.at[dst, v, h or 0], peer(via),
        )

    def got(v, slot, h=None):
        raw_copy(v, slot, slot, 1, h).wait_recv()

    sent = []

    def give(v, src, dst, via, h=None):
        copy = raw_copy(v, src, dst, via, h)
        copy.start()
        sent.append(copy)

    def give_own(v):
        give(v, 0, 2, 2, 0)
        give(v, 0, 4, 4, 1)
        give(v, 0, 1, 1)
        give(v, 0, 2, 2, 1)
        give(v, 0, 4, 4, 0)

    def give_across(v):
        got(v, 2, 0)
        give(v, 2, 6, 4, 0)
        got(v, 4, 1)
        give(v, 4, 6, 2, 1)

    def block_stat(v):
        x = raw[v, pl.ds(0, rows)].astype(f32)
        mean = jnp.sum(x, axis=0, keepdims=True) / rows
        x = x - mean
        stat[0, pl.ds(2 * v, 1)] = mean
        stat[0, pl.ds(2 * v + 1, 1)] = jnp.sum(x * x, axis=0, keepdims=True)

    def stat_copy(r):
        return remote(stat.at[0], stat.at[r], stat_s.at[r], stat_r.at[r], peer(r))

    for v in (1, 0):
        fetch[v].wait()
        block_stat(v)
    pl.semaphore_wait(barrier, DP + jnp.where(is_mid, 1, 0))
    for r in range(DP - 1, 0, -1):
        stat_copy(r).start()
    give_own(1)
    for r in range(1, DP):
        stat_copy(r).wait_recv()
    for v in range(2):
        means = [stat[r, pl.ds(2 * v, 1)] for r in range(DP)]
        mean = sum(means) / DP
        square = sum(stat[r, pl.ds(2 * v + 1, 1)] for r in range(DP))
        square = square + rows * sum((one - mean) * (one - mean) for one in means)
        mean_ref[pl.ds(v, 1)] = mean
        inverse_ref[pl.ds(v, 1)] = lax.rsqrt(square / total_rows + EPSILON)

    def normalize(v, slot):
        x = raw[v, pl.ds(slot * rows, rows)].astype(f32)
        norm[v, pl.ds(slot * rows, rows)] = (
            (x - mean_ref[pl.ds(v, 1)]) * inverse_ref[pl.ds(v, 1)]
        ).astype(bf16)

    chunks = ((1, 0), (1, 1), (1, 2), (1, 3), (0, 0), (0, 1), (0, 2), (0, 3))
    wide = 2 * rows

    def end_copy(k):
        return remote(own_gram.at[k], from_end.at[k], gram_s.at[k], end_r.at[k], inner)

    def mid_copy(k):
        return remote(own_gram.at[k], from_mid.at[k], gram_s.at[k], mid_r.at[k], inner)

    def total_copy(k):
        return remote(gram.at[k], gram.at[k], total_s.at[k], total_r.at[k], outer)

    def own(k):
        v, p = chunks[k]
        own_gram[k] = times_t(norm[v, pl.ds(0, rows)], norm[v, pl.ds(p * wide, wide)]).astype(bf16)

        @pl.when(is_end)
        def _():
            end_copy(k).start()

    def across(k):
        @pl.when(is_mid)
        def _():
            end_copy(k).wait_recv()
            own_gram[k] = (own_gram[k].astype(f32) + from_end[k].astype(f32)).astype(bf16)
            mid_copy(k).start()

    def back_out(k):
        @pl.when(is_mid)
        def _():
            mid_copy(k).wait_recv()
            gram[k] = (own_gram[k].astype(f32) + from_mid[k].astype(f32)).astype(bf16)
            total_copy(k).start()

    def use(k, slots=(0, 1)):
        v, p = chunks[k]

        if slots[0] == 0:
            @pl.when(is_end)
            def _():
                total_copy(k).wait_recv()

        skip, size = slots[0] * rows, len(slots) * rows
        product = jnp.dot(
            gram[k, :, pl.ds(skip, size)], norm[1 - v, pl.ds(p * wide + skip, size)],
            preferred_element_type=f32,
        )
        if p == 0:
            up[1 - v] = product
        else:
            up[1 - v] += product

    def match(p, slots=(0, 1)):
        at = pl.ds(p * wide + slots[0] * rows, len(slots) * rows)
        both = norm[0, at].astype(f32) * norm[1, at].astype(f32)
        both = jnp.sum(both, axis=0, keepdims=True)
        diagonal[pl.ds(0, 1)] = both if p == 0 else diagonal[pl.ds(0, 1)] + both

    def back_copy(v, r):
        return remote(back.at[v, 0], back.at[v, r], back_s.at[v, r], back_r.at[v, r], peer(r))

    def upstream(v):
        diag = diagonal[pl.ds(0, 1)] / total_rows
        slope = 2.0 * (diag - 1.0) - 2.0 * OFF_WEIGHT * diag
        mine = norm[v, pl.ds(0, rows)].astype(f32)
        other = norm[1 - v, pl.ds(0, rows)].astype(f32)
        value = up[v] * (2.0 * OFF_WEIGHT / total_rows) + other * slope
        up[v] = value
        back[v, 0, pl.ds(0, 1)] = jnp.sum(value, axis=0, keepdims=True)
        back[v, 0, pl.ds(1, 1)] = jnp.sum(value * mine, axis=0, keepdims=True)
        for r in range(DP - 1, 0, -1):
            back_copy(v, r).start()

    def through_norm(v):
        for r in range(1, DP):
            back_copy(v, r).wait_recv()
        mean_up = sum(back[v, r, pl.ds(0, 1)] for r in range(DP)) / total_rows
        cross = sum(back[v, r, pl.ds(1, 1)] for r in range(DP)) / total_rows
        mine = norm[v, pl.ds(0, rows)].astype(f32)
        delta[v] = (inverse_ref[pl.ds(v, 1)] * (up[v] - mean_up - mine * cross)).astype(bf16)

    slim = width // PARTS

    def outward(v, j, c):
        return remote(
            part.at[v, j, c], from_outer.at[v, j, c], part_s.at[v, j, c], outer_r.at[v, j, c], inner
        )

    def over(v, j, c):
        return remote(
            part.at[v, j, c], from_inner.at[v, 3 - j, c], part_s.at[v, j, c], inner_r.at[v, 3 - j, c], inner
        )

    def homeward(v, c):
        return remote(
            part.at[v, 0, c], from_inner.at[v, 0, c], part_s.at[v, 0, c], inner_r.at[v, 0, c], outer
        )

    def product(v, j, c):
        block = jnp.where(low, j, MP - 1 - j)
        start = pl.multiple_of(block * width + c * slim, slim)
        return times_t(delta[v], weight[pl.ds(start, slim)])

    def send_out(v):
        @pl.when(is_end)
        def _():
            @pl.loop(0, (MP - 1) * PARTS)
            def _(step):
                j = MP - 1 - lax.div(step, PARTS)
                c = lax.rem(step, PARTS)
                part[v, j, c] = product(v, j, c).astype(bf16)
                outward(v, j, c).start()

    def pass_on(v, j, c):
        mine = product(v, j, c)
        outward(v, j, c).wait_recv()
        part[v, j, c] = (mine + from_outer[v, j, c].astype(f32)).astype(bf16)
        over(v, j, c).start()

    def pass_home(v, c):
        mine = product(v, 0, c)
        over(v, 3, c).wait_recv()
        part[v, 0, c] = (mine + from_inner[v, 0, c].astype(f32)).astype(bf16)
        homeward(v, c).start()

    normalize(1, 0)
    got(1, 1)
    normalize(1, 1)
    own(0)
    give_across(1)
    give_own(0)
    got(1, 2, 1)
    give(1, 2, 3, 1)
    got(1, 4, 0)
    give(1, 4, 5, 1)
    normalize(1, 2)
    normalize(1, 4)
    across(0)
    got(1, 3)
    normalize(1, 3)
    own(1)
    got(1, 5)
    normalize(1, 5)
    own(2)
    back_out(0)
    normalize(0, 0)
    got(0, 1)
    normalize(0, 1)
    got(1, 6, 0)
    got(1, 6, 1)
    give(1, 6, 7, 1)
    normalize(1, 6)
    across(1)
    across(2)
    got(1, 7)
    normalize(1, 7)
    own(3)
    own(4)
    match(0)

    give_across(0)
    back_out(1)
    back_out(2)
    use(0)
    across(3)
    across(4)
    got(0, 2, 1)
    give(0, 2, 3, 1)
    got(0, 4, 0)
    give(0, 4, 5, 1)
    normalize(0, 2)
    normalize(0, 4)
    got(0, 3)
    normalize(0, 3)
    own(5)
    back_out(3)
    use(1)
    got(0, 5)
    normalize(0, 5)
    own(6)
    back_out(4)
    use(2)
    match(1)
    match(2)
    across(5)
    across(6)
    got(0, 6, 0)
    give(0, 6, 7, 1, 0)
    got(0, 6, 1)
    give(0, 6, 7, 1, 1)
    normalize(0, 6)
    match(3, (0,))
    use(3, (0,))
    got(0, 7, 0)
    got(0, 7, 1)
    normalize(0, 7)
    match(3, (1,))
    use(3, (1,))
    upstream(0)
    own(7)
    back_out(5)
    back_out(6)
    use(4)
    load.wait()
    through_norm(0)
    across(7)
    send_out(0)

    back_out(7)
    use(5)
    use(6)
    use(7)
    upstream(1)

    @pl.when(is_mid)
    def _():
        @pl.loop(0, PARTS)
        def _(c):
            pass_on(0, MP - 1, c)

    through_norm(1)
    send_out(1)

    outs = (grad_one_ref, grad_two_ref)

    def all_left():
        for r in range(1, DP):
            stat_copy(r).wait_send()
            for v in range(2):
                back_copy(v, r).wait_send()
        for copy in sent:
            copy.wait_send()
        for k in range(len(chunks)):
            end_copy(k).wait_send()

    def parts_left(v, blocks):
        for j in blocks:
            for c in range(PARTS):
                outward(v, j, c).wait_send()

    @pl.when(is_end)
    def _():
        all_left()
        for v in range(2):
            @pl.loop(0, PARTS)
            def _(c):
                mine = product(v, 0, c)
                homeward(v, c).wait_recv()
                outs[v][:, pl.ds(pl.multiple_of(c * slim, slim), slim)] = (
                    mine + from_inner[v, 0, c].astype(f32)
                ).astype(bf16)

            parts_left(v, (3, 2, 1))

    @pl.when(is_mid)
    def _():
        for v in range(2):
            if v == 1:
                @pl.loop(0, PARTS)
                def _(c):
                    pass_on(v, MP - 1, c)

            @pl.loop(0, PARTS)
            def _(c):
                pass_home(v, c)
                pass_on(v, MP - 2, c)

            if v == 0:
                all_left()
                for k in range(len(chunks)):
                    total_copy(k).wait_send()
            parts_left(v, (3, 0))

            @pl.loop(0, PARTS)
            def _(c):
                mine = product(v, 1, c)
                over(v, 2, c).wait_recv()
                mine = mine + from_inner[v, 1, c].astype(f32)
                outward(v, 1, c).wait_recv()
                outs[v][:, pl.ds(pl.multiple_of(c * slim, slim), slim)] = (
                    mine + from_outer[v, 1, c].astype(f32)
                ).astype(bf16)

            parts_left(v, (2,))


def local_fused(view_one, view_two, proj_weight):
    rows, width = view_one.shape
    bf16, f32 = jnp.bfloat16, jnp.float32
    dma = pltpu.SemaphoreType.DMA
    slim = width // PARTS
    out = jax.ShapeDtypeStruct((rows, width), bf16)
    vmem = pl.BlockSpec(memory_space=pltpu.VMEM)
    return pl.pallas_call(
        fused,
        out_shape=(out, out),
        in_specs=[pl.BlockSpec(memory_space=pltpu.HBM)] * 3,
        out_specs=(vmem, vmem),
        scratch_shapes=[
            pltpu.VMEM(proj_weight.shape, bf16),
            pltpu.VMEM((2, DP * rows, width), bf16),
            pltpu.VMEM((2, DP * rows, width), bf16),
            pltpu.VMEM((DP, 4, width), f32),
            pltpu.VMEM((2, DP, 2, width), f32),
            pltpu.VMEM((8, width), f32),
            pltpu.VMEM((8, width), f32),
            pltpu.VMEM((8, width), f32),
            pltpu.VMEM((2, rows, width), f32),
            pltpu.VMEM((8, rows, 2 * rows), bf16),
            pltpu.VMEM((8, rows, 2 * rows), bf16),
            pltpu.VMEM((8, rows, 2 * rows), bf16),
            pltpu.VMEM((8, rows, 2 * rows), bf16),
            pltpu.VMEM((2, rows, width), bf16),
            pltpu.VMEM((2, MP, PARTS, rows, slim), bf16),
            pltpu.VMEM((2, MP, PARTS, rows, slim), bf16),
            pltpu.VMEM((2, 2, PARTS, rows, slim), bf16),
            dma((2,)),
            dma(()),
            dma((DP,)), dma((DP,)), dma((2, DP)), dma((2, DP)),
            dma((DP, 2, 2)), dma((DP, 2, 2)),
            dma((8,)), dma((8,)), dma((8,)), dma((8,)), dma((8,)),
            dma((2, MP, PARTS)), dma((2, MP, PARTS)), dma((2, 2, PARTS)),
        ],
        compiler_params=pltpu.CompilerParams(
            collective_id=0, has_side_effects=True, vmem_limit_bytes=VMEM_KIB * 1024
        ),
        cost_estimate=pl.CostEstimate(
            flops=4 * rows * width * (2 * DP * rows + MP * width),
            bytes_accessed=2 * (MP * width * width + 4 * rows * width),
            transcendentals=0,
        ),
    )(view_one, view_two, proj_weight)


def contract_rows(left, right):
    return lax.dot_general(
        left, right, (((0,), (0,)), ((), ())), preferred_element_type=jnp.float32
    )


def times_transposed(left, right):
    return lax.dot_general(
        left, right, (((1,), (1,)), ((), ())), preferred_element_type=jnp.float32
    )


def local(view_one, view_two, proj_weight):
    row_count, local_width = view_one.shape
    batch_devices = lax.axis_size("dp")
    total_rows = row_count * batch_devices
    first = view_one.astype(jnp.float32)
    second = view_two.astype(jnp.float32)
    sum_one, sum_two = lax.psum((jnp.sum(first, axis=0), jnp.sum(second, axis=0)), "dp")
    center_one = sum_one / total_rows
    center_two = sum_two / total_rows
    centered_one = first - center_one
    centered_two = second - center_two
    square_one, square_two = lax.psum(
        (
            jnp.sum(centered_one * centered_one, axis=0),
            jnp.sum(centered_two * centered_two, axis=0),
        ),
        "dp",
    )
    variance_one = square_one / total_rows
    variance_two = square_two / total_rows
    inverse_one = lax.rsqrt(variance_one + EPSILON)
    inverse_two = lax.rsqrt(variance_two + EPSILON)
    norm_one = (centered_one * inverse_one).astype(jnp.bfloat16)
    norm_two = (centered_two * inverse_two).astype(jnp.bfloat16)
    whole_two = lax.all_gather(norm_two, "mp", axis=1, tiled=True)
    total_width = whole_two.shape[1]
    block_index = lax.axis_index("mp")
    slab_index = lax.axis_index("dp")
    shard_cols = total_width // batch_devices
    corr_part = contract_rows(norm_one, whole_two)
    corr_shard = lax.psum_scatter(corr_part, "dp", scatter_dimension=1, tiled=True) / total_rows
    row_ids = block_index * local_width + lax.broadcasted_iota(
        jnp.int32, (local_width, shard_cols), 0
    )
    col_ids = slab_index * shard_cols + lax.broadcasted_iota(
        jnp.int32, (local_width, shard_cols), 1
    )
    grad_shard = jnp.where(
        row_ids == col_ids, -2.0 * (1.0 - corr_shard), 2.0 * OFF_WEIGHT * corr_shard
    ).astype(jnp.bfloat16)
    piece = lax.all_gather(grad_shard, "dp", axis=1, tiled=True)
    upper = times_transposed(whole_two, piece)
    fresh = jnp.dot(norm_one, piece, preferred_element_type=jnp.float32)
    up_two = lax.psum_scatter(
        fresh.astype(jnp.bfloat16), "mp", scatter_dimension=1, tiled=True
    ).astype(jnp.float32)
    normal_one = norm_one.astype(jnp.float32)
    normal_two = norm_two.astype(jnp.float32)
    mean_up_one, cross_one, mean_up_two, cross_two = lax.psum(
        (
            jnp.sum(upper, axis=0),
            jnp.sum(upper * normal_one, axis=0),
            jnp.sum(up_two, axis=0),
            jnp.sum(up_two * normal_two, axis=0),
        ),
        "dp",
    )
    delta_one = (
        inverse_one * (upper - mean_up_one / total_rows - normal_one * (cross_one / total_rows))
    ).astype(jnp.bfloat16)
    delta_two = (
        inverse_two * (up_two - mean_up_two / total_rows - normal_two * (cross_two / total_rows))
    ).astype(jnp.bfloat16)
    partial_one = times_transposed(delta_one, proj_weight)
    partial_two = times_transposed(delta_two, proj_weight)
    summed_one, summed_two = (
        lax.psum_scatter(
            partial_one.astype(jnp.bfloat16), "mp", scatter_dimension=1, tiled=True
        ).astype(jnp.float32),
        lax.psum_scatter(
            partial_two.astype(jnp.bfloat16), "mp", scatter_dimension=1, tiled=True
        ).astype(jnp.float32),
    )
    return (summed_one.astype(jnp.bfloat16), summed_two.astype(jnp.bfloat16))


def solution(mesh):
    placed = (P("dp", "mp"), P("dp", "mp"), P(None, "mp"))

    def whole(view_one, view_two, proj_weight):
        batch, features = view_one.shape
        suits = dict(mesh.shape) == {"dp": DP, "mp": MP}
        suits = suits and batch % (DP * 128) == 0 and 2 * batch <= features and features <= 4096
        return jax.shard_map(
            local_fused if suits else local,
            mesh=mesh, in_specs=placed, out_specs=(P("dp", "mp"), P("dp", "mp")), check_vma=False,
        )(view_one, view_two, proj_weight)

    return whole
```
